128 devices in a mesh: member: 8 (over z_lo, x), grid: 16 (over y, z_hi, core).
Axes of the slice: x: 4, y: 4, z: 4 (z_hi: 2, z_lo: 2; z = z_hi * 2 + z_lo), core: 2. Of those that a mesh axis runs over, the one named last changes fastest.
Arguments:
- latent: bfloat16 [8, 32768, 1024], P('member', 'grid'), may hold values from -6 to 6
- w_in: bfloat16 [1024, 1024], P(('member', 'grid')), may hold values from -0.1875 to 0.1875
- b_in: float32 [1024], replicated, may hold values from -3 to 3
- w_out: bfloat16 [100, 1024], replicated, may hold values from -0.1875 to 0.1875
- b_out: float32 [100], replicated, may hold values from -3 to 3
- targets: float32 [100, 32768], P(None, 'grid'), may hold values from -6 to 6
- var_weight: float32 [100], replicated, may hold values from 0.5 to 5
- plan: int32 [3, 8], replicated, may hold values from 0 to 7, as said below
Outputs:
- loss: float32 [], replicated
- grad_latent: bfloat16 [8, 32768, 1024], P('member', 'grid')
- grad_w_in: float32 [1024, 1024], P(('member', 'grid'))
- grad_b_in: float32 [1024], replicated
- grad_w_out: float32 [100, 1024], replicated
- grad_b_out: float32 [100], replicated
The draws below stay inside these ranges and needn't reach their ends.
Inputs may be any that keep to these rules, and one draw needn't show every extreme that they name: `plan`: each row is a perfect pairing of the 8 members: no member is its own partner, the partner of a member's partner is the member, and no pair occurs in two rows.
All inputs are finite; a program needn't handle non-finite values.
Results may differ from the reference program's by a relative error of at most 0.0095.
Values may be sent and summed in bfloat16 or wider, within the bound.
No kernel may reach another device: no remote copies, remote signals or barrier semaphores. Data moves between devices by JAX's collectives and lax.ppermute only.
A program may use at most 128 MiB of HBM per device.

```python
import math
import jax
import jax.numpy as jnp
from jax import lax

L = 1024
V = 100
ROUNDS = 3
MEMBERS = 8
POINTS = 32768


def draw_plan(key, part):
    first_key, second_key = jax.random.split(jax.random.fold_in(key, 7))
    relabel = jax.random.permutation(first_key, MEMBERS).astype(jnp.int32)
    chosen = jax.random.permutation(second_key, MEMBERS - 1)[:ROUNDS].astype(jnp.int32)
    labels = jnp.arange(MEMBERS, dtype=jnp.int32)[None, :]
    rounds = chosen[:, None]
    partner = (2 * rounds - labels) % (MEMBERS - 1)
    partner = jnp.where(labels == rounds, MEMBERS - 1, partner)
    partner = jnp.where(labels == MEMBERS - 1, rounds, partner)
    mapped = relabel[partner]
    table = jnp.zeros((ROUNDS, MEMBERS), jnp.int32).at[:, relabel].set(mapped)
    return table.astype(jnp.int32)


def levels(stream_key, extent, cuts, least, largest):
    factor_of = 1.0
    for dim, parts in cuts:
        steps = jax.random.uniform(jax.random.fold_in(jax.random.fold_in(stream_key, 6), dim), (parts,), jnp.float32, least / len(cuts), largest / len(cuts))
        factor_of = factor_of * jnp.repeat(jnp.exp(steps), extent[dim] // parts).reshape((-1,) + (1,) * (len(extent) - 1 - dim))
    return factor_of


def normal_values(own_key, extent, width, most, pieces=(), kind=jnp.bfloat16):
    level = levels(own_key, extent, pieces, -0.22, 0.18) if pieces else 1.0
    entries = jax.random.normal(own_key, extent, jnp.float32) * width * level
    return jnp.minimum(jnp.maximum(entries, -most), most).astype(kind)


def setup_inputs(seed: int = 0) -> dict:
    key_list = jax.random.split(jax.random.key(seed), 9)
    return {
        "latent": normal_values(key_list[0], (MEMBERS, POINTS, L), 1.0, 6.0, ((0, 8), (1, 16))),
        "w_in": normal_values(key_list[1], (L, L), L ** -0.5, 0.1875, ((0, 128),)),
        "b_in": normal_values(key_list[2], (L,), 0.5, 3.0, (), jnp.float32),
        "w_out": normal_values(key_list[3], (V, L), L ** -0.5, 0.1875),
        "b_out": normal_values(key_list[4], (V,), 0.5, 3.0, (), jnp.float32),
        "targets": normal_values(key_list[5], (V, POINTS), 1.0, 6.0, ((1, 16),), jnp.float32),
        "var_weight": jnp.clip(jnp.exp(jax.random.uniform(key_list[6], (V,), jnp.float32, math.log(0.5), math.log(5.0))), 0.5, 5.0),
        "plan": draw_plan(jax.random.fold_in(key_list[8], 71), 0),
    }


DELTA = 0.25

def reference(latent, w_in, b_in, w_out, b_out, targets, var_weight, plan):
    place = jnp.arange(POINTS).astype(jnp.float32)
    area = jnp.cos(1.4 * (place + 0.5) / POINTS)
    scale_map = area[None, :] * var_weight[:, None]

    def forward(hidden_in):
        pre = jnp.dot(hidden_in, w_in, preferred_element_type=jnp.float32) + b_in[None, :]
        act = jax.nn.gelu(pre).astype(jnp.bfloat16)
        field = jnp.dot(w_out, act.T, preferred_element_type=jnp.float32) + b_out[:, None]
        return field
    fields = lax.map(forward, latent)

    def member_step(carry, member):
        acc_w1, acc_w2, acc_b1, acc_b2, acc_loss = carry
        hidden_in = latent[member]
        field = fields[member]
        others = fields[plan[:, member]]
        diff = field[None] - others
        root = jnp.sqrt(diff * diff + DELTA * DELTA)
        pairs = lax.optimization_barrier(jnp.sum(diff / root, axis=0))
        spread = lax.optimization_barrier(jnp.sum(root - DELTA, axis=0))
        miss = field - targets
        miss_root = jnp.sqrt(miss * miss + DELTA * DELTA)
        cot = scale_map * (miss / miss_root - pairs / ROUNDS)
        terms = scale_map * (miss_root - DELTA - spread / (2.0 * ROUNDS))
        cot_b = cot.astype(jnp.bfloat16)
        pre = jnp.dot(hidden_in, w_in, preferred_element_type=jnp.float32) + b_in[None, :]
        act = jax.nn.gelu(pre).astype(jnp.bfloat16)
        dact = jnp.dot(cot_b.T, w_out, preferred_element_type=jnp.float32)
        _, pull = jax.vjp(jax.nn.gelu, pre)
        dpre = pull(dact)[0]
        dpre_b = dpre.astype(jnp.bfloat16)
        grad_hidden = jnp.dot(dpre_b, w_in.T, preferred_element_type=jnp.float32).astype(jnp.bfloat16)
        acc_w1 = acc_w1 + jnp.dot(hidden_in.T, dpre_b, preferred_element_type=jnp.float32)
        acc_w2 = acc_w2 + jnp.dot(cot_b, act, preferred_element_type=jnp.float32)
        acc_b1 = acc_b1 + lax.optimization_barrier(jnp.sum(dpre, axis=0))
        acc_b2 = acc_b2 + lax.optimization_barrier(jnp.sum(cot, axis=1))
        acc_loss = acc_loss + jnp.sum(terms)
        return ((acc_w1, acc_w2, acc_b1, acc_b2, acc_loss), grad_hidden)
    start = (jnp.zeros((L, L), jnp.float32), jnp.zeros((V, L), jnp.float32), jnp.zeros((L,), jnp.float32), jnp.zeros((V,), jnp.float32), jnp.zeros((), jnp.float32))
    (acc_w1, acc_w2, acc_b1, acc_b2, acc_loss), grad_latent = lax.scan(member_step, start, jnp.arange(MEMBERS).astype(jnp.int32))
    kappa = 4.0 / jnp.sqrt(jnp.float32(MEMBERS * POINTS))
    loss = acc_loss / (MEMBERS * POINTS * V)
    return (loss, grad_latent, acc_w1 * kappa, acc_b1 * kappa, acc_w2 * kappa, acc_b2 * kappa)
```

```python
import jax
import jax.numpy as jnp
from jax import lax
from jax.sharding import PartitionSpec as P

DELTA = 0.25
BOTH = ("member", "grid")


def shards(latent, w_in, b_in, w_out, b_out, targets, var_weight, plan):
    hidden_in = latent[0]
    points, width = hidden_in.shape
    half = width // 2
    variables = w_out.shape[0]
    rounds, members = plan.shape
    member = lax.axis_index("member")
    grid_index = lax.axis_index("grid")
    grid_count = lax.axis_size("grid")
    devices = members * grid_count
    rows = w_in.shape[0]
    total = points * grid_count
    block = points // members
    core = lax.rem(grid_index, 2)
    swap = [(i, i ^ 1) for i in range(devices)]

    halves = jnp.stack([w_in[:, :half], w_in[:, half:]])
    send = jnp.broadcast_to(halves[None], (devices // 2, 2, rows, half))
    w_mine = lax.all_to_all(send.reshape(devices * rows, half), BOTH, 0, 0, tiled=True)
    w_other = lax.ppermute(w_mine, BOTH, swap)

    def part(a, which):
        return lax.dynamic_slice_in_dim(a, which * half, half, a.ndim - 1)

    w_halves = (w_mine, w_other)
    b_halves = (part(b_in, core), part(b_in, 1 - core))
    o_halves = (part(w_out, core), part(w_out, 1 - core))

    pres, acts, field = [], [], b_out[:, None]
    for w, b, o in zip(w_halves, b_halves, o_halves):
        pre = jnp.dot(hidden_in, w, preferred_element_type=jnp.float32) + b[None, :]
        act = jax.nn.gelu(pre).astype(jnp.bfloat16)
        field = field + jnp.dot(o, act.T, preferred_element_type=jnp.float32)
        pres.append(pre)
        acts.append(act)

    out = field.reshape(variables, members, block).transpose(1, 0, 2)
    fields = lax.all_to_all(out, "member", 0, 0, tiled=True)
    place = grid_index * points + member * block + jnp.arange(block, dtype=jnp.int32)
    area = jnp.cos(1.4 * (place.astype(jnp.float32) + 0.5) / total)
    scale_map = area[None, :] * var_weight[:, None]
    target = lax.dynamic_slice_in_dim(targets, member * block, block, 1)
    slopes, spreads = 0.0, 0.0
    for r in range(rounds):
        partners = [lax.dynamic_index_in_dim(fields, plan[r, m], 0) for m in range(members)]
        diff = fields - jnp.concatenate(partners)
        root = jnp.sqrt(diff * diff + DELTA * DELTA)
        slopes = slopes + diff / root
        spreads = spreads + (root - DELTA)
    miss = fields - target[None]
    miss_root = jnp.sqrt(miss * miss + DELTA * DELTA)
    cot = scale_map[None] * (miss / miss_root - slopes / rounds)
    terms = scale_map[None] * (miss_root - DELTA - spreads / (2.0 * rounds))
    sum_b2 = jnp.sum(cot, axis=(0, 2))
    sum_loss = jnp.sum(terms)
    back = lax.all_to_all(cot.astype(jnp.bfloat16), "member", 0, 0, tiled=True)
    cot_b = back.transpose(1, 0, 2).reshape(variables, points)

    grads1, grads2, sums1, dpres = [], [], [], []
    for pre, act, o in zip(pres, acts, o_halves):
        dact = jnp.dot(cot_b.T, o, preferred_element_type=jnp.float32)
        _, pull = jax.vjp(jax.nn.gelu, pre)
        dpre = pull(dact)[0]
        dpre_b = dpre.astype(jnp.bfloat16)
        dpres.append(dpre_b)
        grads1.append(jnp.dot(hidden_in.T, dpre_b, preferred_element_type=jnp.float32))
        grads2.append(jnp.dot(cot_b, act, preferred_element_type=jnp.float32))
        sums1.append(jnp.sum(dpre, axis=0))
    grad_hidden = sum(
        jnp.dot(d, w.T, preferred_element_type=jnp.float32) for d, w in zip(dpres, w_halves)
    ).astype(jnp.bfloat16)

    tail = jnp.concatenate([sum_b2, sum_loss[None], jnp.zeros((half - variables - 1,), jnp.float32)])
    def table(i):
        t = jnp.concatenate([grads2[i], sums1[i][None], (tail if i == 0 else 0 * tail)[None]])
        t = jnp.pad(t, ((0, devices - t.shape[0]), (0, 0)))
        t = t.reshape(16, 8, 8, half // 8).transpose(0, 2, 1, 3)
        return t.reshape(devices * 8, half // 8)

    def whole(i):
        return jnp.concatenate([grads1[i], table(i)], axis=1)

    got = lax.ppermute(whole(1).astype(jnp.bfloat16), BOTH, swap)
    mine = (whole(0) + got.astype(jnp.float32)).astype(jnp.bfloat16)
    parts = lax.all_to_all(mine, BOTH, 0, 0, tiled=True)
    summed = jnp.sum(parts.reshape(devices // 2, 2, rows, -1).astype(jnp.float32), axis=0)
    own_rows = jnp.concatenate([summed[0, :, :half], summed[1, :, :half]], axis=1)
    small = jnp.concatenate([summed[0, :, half:], summed[1, :, half:]], axis=1)
    spread_small = jnp.broadcast_to(small[None], (devices,) + small.shape)
    everyone = lax.all_to_all(spread_small, BOTH, 0, 0)
    tables = everyone.reshape(16, 8, 8, 2, half // 8).transpose(0, 2, 3, 1, 4).reshape(devices, width)
    tails = tables[variables + 1, :half] + tables[variables + 1, half:]
    kappa = 4.0 / jnp.sqrt(jnp.float32(members * total))
    loss = tails[variables] / (members * total * variables)
    return (
        loss,
        grad_hidden[None],
        own_rows * kappa,
        tables[variables] * kappa,
        tables[:variables] * kappa,
        tails[:variables] * kappa,
    )


def solution(mesh):
    placed = (
        P("member", "grid", None),
        P(BOTH, None),
        P(),
        P(),
        P(),
        P(None, "grid"),
        P(),
        P(),
    )
    return jax.shard_map(
        shards,
        mesh=mesh,
        in_specs=placed,
        out_specs=(P(), P("member", "grid", None), P(BOTH, None), P(), P(), P()),
        check_vma=False,
    )
```

```python
import jax
import jax.numpy as jnp
from jax import lax
from jax.experimental import pallas as pl
from jax.experimental.pallas import tpu as pltpu
from jax.sharding import PartitionSpec as P

DELTA = 0.25
BOTH = ("member", "grid")
VMEM_BYTES = 48 << 20


def pair_kernel(plan_ref, f_ref, t_ref, s_ref, cot_ref, b2_ref, l_ref):
    n, v, blk = f_ref.shape
    rounds = plan_ref.shape[0]
    vp = cot_ref.shape[1]
    D = DELTA
    b2_ref[...] = jnp.zeros_like(b2_ref); l_ref[...] = jnp.zeros_like(l_ref)
    cot_ref[...] = jnp.zeros_like(cot_ref)
    RB = 16
    def body(m, _):
        for r0 in range(0, v, RB):
            rs = slice(r0, min(r0+RB, v))
            f = f_ref[m, rs, :]
            sc = s_ref[rs, :]
            d = f - t_ref[rs, :]
            q = d*d + D*D
            inv = lax.rsqrt(q)
            slope = d*inv
            spread = q*inv - D
            ps = jnp.zeros_like(f); pr = jnp.zeros_like(f)
            for r in range(rounds):
                x = f - f_ref[plan_ref[r, m], rs, :]
                y = x*x + D*D
                iv = lax.rsqrt(y)
                ps += x*iv
                pr += y*iv - D
            cot = sc*(slope - ps*(1.0/rounds))
            b2_ref[rs, :] += cot
            l_ref[rs, :] += sc*(spread - pr*(0.5/rounds))
            h = min(RB, v-r0)
            cb = cot.astype(jnp.bfloat16)
            if h < RB:
                cb = jnp.concatenate([cb.astype(jnp.float32), jnp.zeros((RB-h, blk), jnp.float32)]).astype(jnp.bfloat16)
            cot_ref[m, r0:r0+RB, :] = cb
        return 0
    lax.fori_loop(0, n, body, 0)

def pair(plan, f, t, s):
    n, v, blk = f.shape
    vp = -(-v//16)*16
    vm = pl.BlockSpec(memory_space=pltpu.VMEM)
    return pl.pallas_call(pair_kernel, in_specs=[pl.BlockSpec(memory_space=pltpu.SMEM), vm, vm, vm], out_specs=[vm]*3,
        out_shape=[jax.ShapeDtypeStruct((n,vp,blk),jnp.bfloat16), jax.ShapeDtypeStruct((v,blk),jnp.float32), jax.ShapeDtypeStruct((v,blk),jnp.float32)],
        compiler_params=pltpu.CompilerParams(vmem_limit_bytes=VMEM_BYTES), name="pair_terms")(plan,f,t,s)


def shards(latent, w_in, b_in, w_out, b_out, targets, var_weight, plan):
    hidden_in = latent[0]
    points, width = hidden_in.shape
    half = width // 2
    variables = w_out.shape[0]
    rounds, members = plan.shape
    member = lax.axis_index("member")
    grid_index = lax.axis_index("grid")
    grid_count = lax.axis_size("grid")
    devices = members * grid_count
    rows = w_in.shape[0]
    total = points * grid_count
    block = points // members
    core = lax.rem(grid_index, 2)
    swap = [(i, i ^ 1) for i in range(devices)]

    halves = jnp.stack([w_in[:, :half], w_in[:, half:]])
    send = jnp.broadcast_to(halves[None], (devices // 2, 2, rows, half))
    w_mine = lax.all_to_all(send.reshape(devices * rows, half), BOTH, 0, 0, tiled=True)
    w_other = lax.ppermute(w_mine, BOTH, swap)

    def part(a, which):
        return lax.dynamic_slice_in_dim(a, which * half, half, a.ndim - 1)

    w_halves = (w_mine, w_other)
    b_halves = (part(b_in, core), part(b_in, 1 - core))
    o_halves = (part(w_out, core), part(w_out, 1 - core))

    pres, acts, field = [], [], b_out[:, None]
    for w, b, o in zip(w_halves, b_halves, o_halves):
        pre = jnp.dot(hidden_in, w, preferred_element_type=jnp.float32) + b[None, :]
        act = jax.nn.gelu(pre).astype(jnp.bfloat16)
        field = field + jnp.dot(o, act.T, preferred_element_type=jnp.float32)
        pres.append(pre)
        acts.append(act)

    out = field.reshape(variables, members, block).transpose(1, 0, 2)
    fields = lax.all_to_all(out, "member", 0, 0, tiled=True)
    place = grid_index * points + member * block + jnp.arange(block, dtype=jnp.int32)
    area = jnp.cos(1.4 * (place.astype(jnp.float32) + 0.5) / total)
    scale_map = area[None, :] * var_weight[:, None]
    target = lax.dynamic_slice_in_dim(targets, member * block, block, 1)
    cot, b2_terms, loss_terms = pair(plan, fields, target, scale_map)
    sum_b2 = jnp.sum(b2_terms, axis=1)
    sum_loss = jnp.sum(loss_terms)
    back = lax.all_to_all(cot, "member", 0, 0, tiled=True)
    cot_b = back.transpose(1, 0, 2).reshape(-1, points)
    extra = cot_b.shape[0] - variables
    o_halves = [jnp.pad(o, ((0, extra), (0, 0))) for o in o_halves]

    grads1, grads2, sums1, dpres = [], [], [], []
    for pre, act, o in zip(pres, acts, o_halves):
        dact = jnp.dot(cot_b.T, o, preferred_element_type=jnp.float32)
        _, pull = jax.vjp(jax.nn.gelu, pre)
        dpre = pull(dact)[0]
        dpre_b = dpre.astype(jnp.bfloat16)
        dpres.append(dpre_b)
        grads1.append(jnp.dot(hidden_in.T, dpre_b, preferred_element_type=jnp.float32))
        grads2.append(jnp.dot(cot_b, act, preferred_element_type=jnp.float32))
        sums1.append(jnp.sum(dpre, axis=0))
    grad_hidden = sum(
        jnp.dot(d, w.T, preferred_element_type=jnp.float32) for d, w in zip(dpres, w_halves)
    ).astype(jnp.bfloat16)

    tail = jnp.concatenate([sum_b2, sum_loss[None], jnp.zeros((half - variables - 1,), jnp.float32)])
    def table(i):
        t = jnp.concatenate([grads2[i][:variables], sums1[i][None], (tail if i == 0 else 0 * tail)[None]])
        t = jnp.pad(t, ((0, devices - t.shape[0]), (0, 0)))
        t = t.reshape(16, 8, 8, half // 8).transpose(0, 2, 1, 3)
        return t.reshape(devices * 8, half // 8)

    def whole(i):
        return jnp.concatenate([grads1[i], table(i)], axis=1)

    got = lax.ppermute(whole(1).astype(jnp.bfloat16), BOTH, swap)
    mine = (whole(0) + got.astype(jnp.float32)).astype(jnp.bfloat16)
    parts = lax.all_to_all(mine, BOTH, 0, 0, tiled=True)
    summed = jnp.sum(parts.reshape(devices // 2, 2, rows, -1).astype(jnp.float32), axis=0)
    own_rows = jnp.concatenate([summed[0, :, :half], summed[1, :, :half]], axis=1)
    small = jnp.concatenate([summed[0, :, half:], summed[1, :, half:]], axis=1)
    spread_small = jnp.broadcast_to(small[None], (devices,) + small.shape)
    everyone = lax.all_to_all(spread_small, BOTH, 0, 0)
    tables = everyone.reshape(16, 8, 8, 2, half // 8).transpose(0, 2, 3, 1, 4).reshape(devices, width)
    tails = tables[variables + 1, :half] + tables[variables + 1, half:]
    kappa = 4.0 / jnp.sqrt(jnp.float32(members * total))
    loss = tails[variables] / (members * total * variables)
    return (
        loss,
        grad_hidden[None],
        own_rows * kappa,
        tables[variables] * kappa,
        tables[:variables] * kappa,
        tails[:variables] * kappa,
    )


def solution(mesh):
    placed = (
        P("member", "grid", None),
        P(BOTH, None),
        P(),
        P(),
        P(),
        P(None, "grid"),
        P(),
        P(),
    )
    return jax.shard_map(
        shards,
        mesh=mesh,
        in_specs=placed,
        out_specs=(P(), P("member", "grid", None), P(BOTH, None), P(), P(), P()),
        check_vma=False,
    )
```

```python
import math

import jax
import jax.numpy as jnp
from jax import lax
from jax.experimental import pallas as pl
from jax.experimental.pallas import tpu as pltpu
from jax.sharding import PartitionSpec as P

DELTA = 0.25
BOTH = ("member", "grid")
VMEM_BYTES = 60 << 20
VMEM_SMALL = 24 << 20


GELU_A = 0.7978845608028654
GELU_B = 0.044715
WHOLE = pl.BlockSpec(memory_space=pltpu.VMEM)
HBM = pl.BlockSpec(memory_space=pltpu.HBM)


def shape(dims, kind):
    return jax.ShapeDtypeStruct(dims, kind)


def cost(flops, moved, special=0):
    return pl.CostEstimate(flops=flops, bytes_accessed=moved, transcendentals=special)


def load(src, dst, sem):
    copy = pltpu.make_async_copy(src, dst, sem)
    copy.start()
    return copy


def forward_kernel(first, parts, lat, w, b, o, extra, f_ref):
    points = lat.shape[0]
    half = w.shape[1]
    tile = points // parts
    rows, block = f_ref.shape[1:]
    for i in range(parts):
        sl = slice(i * tile, (i + 1) * tile)
        f = None
        for n in range(0, half, 256):
            cols = slice(n, n + 256)
            pre = jnp.dot(lat[sl, :], w[:, cols], preferred_element_type=jnp.float32) + b[:, cols]
            t = jnp.tanh(pre * (GELU_A + (GELU_A * GELU_B) * (pre * pre)))
            act = (pre * (0.5 + 0.5 * t)).astype(jnp.bfloat16)
            g = lax.dot_general(
                o[:, cols], act, (((1,), (1,)), ((), ())), preferred_element_type=jnp.float32
            )
            f = g if f is None else f + g
        for q in range(tile // block):
            at = i * (tile // block) + q
            piece = f[:rows, q * block : (q + 1) * block]
            f_ref[at] = piece + (extra[...] if first else extra[at])


def forward_half(first, lat, w, b, o, extra, rows, blocks):
    points, width = lat.shape
    half = w.shape[1]
    return pl.pallas_call(
        lambda *refs: forward_kernel(first, 4, *refs),
        in_specs=[WHOLE] * 5,
        out_specs=WHOLE,
        out_shape=shape((blocks, rows, points // blocks), jnp.float32),
        compiler_params=pltpu.CompilerParams(vmem_limit_bytes=VMEM_SMALL),
        cost_estimate=cost(2 * points * half * (width + rows), points * 2 * width, points * half),
        name="forward_half",
    )(lat, w, b, o, extra)


def slope_kernel(parts, lat_ref, w_ref, b, act_ref, g_ref, act_v, g_v, lat, w, sems, out_sems):
    points = lat.shape[0]
    half = w.shape[1]
    tile = points // parts
    slices = [slice(i * tile, (i + 1) * tile) for i in range(parts)]

    def fetch(i):
        return load(lat_ref.at[slices[i]], lat.at[slices[i]], sems.at[i])

    ready_w = load(w_ref, w, sems.at[parts])
    ready = [fetch(0)]
    ready_w.wait()
    out = []
    for i, sl in enumerate(slices):
        ready[i].wait()
        if i + 1 < parts:
            ready.append(fetch(i + 1))
        for n in range(0, half, 256):
            cols = slice(n, n + 256)
            pre = jnp.dot(lat[sl, :], w[:, cols], preferred_element_type=jnp.float32) + b[:, cols]
            sq = pre * pre
            t = jnp.tanh(pre * (GELU_A + (GELU_A * GELU_B) * sq))
            gate = 0.5 + 0.5 * t
            act_v[sl, cols] = (pre * gate).astype(jnp.bfloat16)
            inner = (0.5 * pre) * (1.0 - t * t) * (GELU_A + (3.0 * GELU_A * GELU_B) * sq)
            g_v[sl, cols] = (gate + inner).astype(jnp.bfloat16)
        out.append(load(act_v.at[sl], act_ref.at[sl], out_sems.at[2 * i]))
        out.append(load(g_v.at[sl], g_ref.at[sl], out_sems.at[2 * i + 1]))
    for copy in out:
        copy.wait()


def slope_half(lat, w, b):
    points, width = lat.shape
    half = w.shape[1]
    parts = 4
    return pl.pallas_call(
        lambda *refs: slope_kernel(parts, *refs),
        in_specs=[HBM] * 2 + [WHOLE],
        out_specs=[HBM] * 2,
        out_shape=[shape((points, half), jnp.bfloat16)] * 2,
        scratch_shapes=[
            pltpu.VMEM((points, half), jnp.bfloat16),
            pltpu.VMEM((points, half), jnp.bfloat16),
            pltpu.VMEM((points, width), jnp.bfloat16),
            pltpu.VMEM((width, half), jnp.bfloat16),
            pltpu.SemaphoreType.DMA((parts + 1,)),
            pltpu.SemaphoreType.DMA((2 * parts,)),
        ],
        compiler_params=pltpu.CompilerParams(vmem_limit_bytes=VMEM_BYTES),
        cost_estimate=cost(2 * points * half * width, points * (2 * width + 4 * half), points * half),
        name="slope_half",
    )(lat, w, b)


def backward_kernel(variables, parts, *refs):
    cot_ref, g_ref, lat_ref, act_ref, o, tail, dpre_ref, pack_ref = refs[:8]
    cot, g, lat, act, dpre_v, pack, table, sems, out_sems = refs[8:]
    blocks, rows, block = cot.shape
    points, half = g.shape
    width = lat.shape[1]
    kind = pack.dtype
    tile = points // parts
    cut = width // parts
    slices = [slice(i * tile, (i + 1) * tile) for i in range(parts)]

    def fetch(i):
        sl = slices[i]
        return (
            load(g_ref.at[sl], g.at[sl], sems.at[1 + 2 * i]),
            load(act_ref.at[sl], act.at[sl], sems.at[2 + 2 * i]),
        )

    def fetch_lat(i):
        cols = pl.ds(i * cut, cut)
        return load(lat_ref.at[:, cols], lat.at[:, cols], sems.at[1 + 2 * parts + i])

    ready_cot = load(cot_ref, cot, sems.at[0])
    ready = [fetch(0), fetch(1)]
    ready_lat = []
    ready_cot.wait()
    b1, w2 = None, None
    out = []
    for i in range(parts):
        for copy in ready[i]:
            copy.wait()
        if i + 2 < parts:
            ready.append(fetch(i + 2))
        else:
            ready_lat.append(fetch_lat(i + 2 - parts))
        for q in range(i * blocks // parts, (i + 1) * blocks // parts):
            sl = slice(q * block, (q + 1) * block)
            dact = lax.dot_general(
                cot[q], o[...], (((0,), (0,)), ((), ())), preferred_element_type=jnp.float32
            )
            dpre = dact * g[sl, :].astype(jnp.float32)
            dpre_v[sl, :] = dpre.astype(jnp.bfloat16)
            s = jnp.sum(dpre.reshape(-1, 8, half), axis=0)
            b1 = s if b1 is None else b1 + s
            a = jnp.dot(cot[q], act[sl, :], preferred_element_type=jnp.float32)
            w2 = a if w2 is None else w2 + a
        sl = slice(i * tile, (i + 1) * tile)
        out.append(load(dpre_v.at[sl], dpre_ref.at[sl], out_sems.at[i]))
    table[...] = jnp.zeros_like(table)
    table[:rows, :] = w2
    table[variables : variables + 1, :] = jnp.sum(b1, axis=0, keepdims=True)
    if kind == jnp.float32:
        table[variables + 1 : variables + 2, : tail.shape[1]] = tail[...]
    side = half // 8
    lanes = half // (2 * side)
    pack[:, half + side :] = jnp.zeros((width, 128 - side), kind)
    for i in range(parts):
        ready_lat[i].wait()
        if i + 2 < parts:
            ready_lat.append(fetch_lat(i + 2))
        sl = slice(i * cut, (i + 1) * cut)
        pack[sl, :half] = lax.dot_general(
            lat[:, sl], dpre_v[...], (((0,), (0,)), ((), ())), preferred_element_type=jnp.float32
        ).astype(kind)
        for unit in range(i * cut // 16, (i + 1) * cut // 16):
            r, c = unit // lanes, unit % lanes
            piece = table[8 * r : 8 * r + 8, 2 * side * c : 2 * side * (c + 1)]
            both = jnp.concatenate([piece[:, :side], piece[:, side:]], axis=0)
            pack[16 * unit : 16 * unit + 16, half : half + side] = both.astype(kind)
        out.append(load(pack.at[sl], pack_ref.at[sl], out_sems.at[parts + i]))
    for copy in out:
        copy.wait()


def backward_half(cot, o, g, lat, act, tail, variables, kind):
    blocks, rows, block = cot.shape
    points, half = g.shape
    width = lat.shape[1]
    parts = 4
    return pl.pallas_call(
        lambda *refs: backward_kernel(variables, parts, *refs),
        in_specs=[HBM] * 4 + [WHOLE] * 2,
        out_specs=[HBM] * 2,
        out_shape=[shape((points, half), jnp.bfloat16), shape((width, half + 128), kind)],
        scratch_shapes=[
            pltpu.VMEM(cot.shape, jnp.bfloat16),
            pltpu.VMEM(g.shape, jnp.bfloat16),
            pltpu.VMEM(lat.shape, jnp.bfloat16),
            pltpu.VMEM(act.shape, jnp.bfloat16),
            pltpu.VMEM((points, half), jnp.bfloat16),
            pltpu.VMEM((width, half + 128), kind),
            pltpu.VMEM((width // 8, half), jnp.float32),
            pltpu.SemaphoreType.DMA((1 + 3 * parts,)),
            pltpu.SemaphoreType.DMA((2 * parts,)),
        ],
        compiler_params=pltpu.CompilerParams(vmem_limit_bytes=VMEM_BYTES),
        cost_estimate=cost(2 * points * half * (width + 2 * rows), points * (2 * width + 6 * half)),
        name="backward_half",
    )(cot, g, lat, act, o, tail)


def finish_kernel(kappa, all_ref, w2_ref, b1_ref, tail_ref):
    variables, width = w2_ref.shape
    half = width // 2
    lanes = half // 128
    side = 64
    for r in range(-(-(variables + 2) // 8)):
        for c in range(lanes):
            a = all_ref[r * 2 * lanes + 2 * c]
            b = all_ref[r * 2 * lanes + 2 * c + 1]
            for h in range(2):
                piece = jnp.concatenate(
                    [a[:, h * side : (h + 1) * side], b[:, h * side : (h + 1) * side]], axis=1
                )
                cols = slice(h * half + 128 * c, h * half + 128 * (c + 1))
                low = 8 * r
                keep = min(8, variables - low)
                if keep > 0:
                    w2_ref[low : low + keep, cols] = piece[:keep] * kappa
                at = variables - low
                if 0 <= at < 8:
                    b1_ref[:, cols] = piece[at : at + 1] * kappa
                at = variables + 1 - low
                if 0 <= at < 8:
                    tail_ref[:, cols] = piece[at : at + 1]


def finish(everyone, variables, width, kappa):
    return pl.pallas_call(
        lambda *refs: finish_kernel(kappa, *refs),
        in_specs=[WHOLE],
        out_specs=[WHOLE] * 3,
        out_shape=[
            shape((variables, width), jnp.float32),
            shape((1, width), jnp.float32),
            shape((1, width), jnp.float32),
        ],
        compiler_params=pltpu.CompilerParams(vmem_limit_bytes=VMEM_SMALL),
        name="finish",
    )(everyone)


def pair_kernel(plan_ref, f_ref, t_ref, s_ref, cot_ref, tail_ref, b2_ref, l_ref):
    n, v, blk = f_ref.shape
    rounds = plan_ref.shape[0]
    vp = cot_ref.shape[1]
    D = DELTA
    b2_ref[...] = jnp.zeros_like(b2_ref); l_ref[...] = jnp.zeros_like(l_ref)
    cot_ref[...] = jnp.zeros_like(cot_ref)
    RB = 16
    def body(m, _):
        for r0 in range(0, v, RB):
            rs = slice(r0, min(r0+RB, v))
            f = f_ref[m, rs, :]
            sc = s_ref[rs, :]
            d = f - t_ref[rs, :]
            q = d*d + D*D
            inv = lax.rsqrt(q)
            slope = d*inv
            spread = q*inv - D
            ps = jnp.zeros_like(f); pr = jnp.zeros_like(f)
            for r in range(rounds):
                x = f - f_ref[plan_ref[r, m], rs, :]
                y = x*x + D*D
                iv = lax.rsqrt(y)
                ps += x*iv
                pr += y*iv - D
            cot = sc*(slope - ps*(1.0/rounds))
            b2_ref[rs, :] += cot
            l_ref[rs, :] += sc*(spread - pr*(0.5/rounds))
            h = min(RB, v-r0)
            cb = cot.astype(jnp.bfloat16)
            if h < RB:
                cb = jnp.concatenate([cb.astype(jnp.float32), jnp.zeros((RB-h, blk), jnp.float32)]).astype(jnp.bfloat16)
            cot_ref[m, r0:r0+RB, :] = cb
        return 0
    lax.fori_loop(0, n, body, 0)
    tail_ref[:, :128] = jnp.sum(b2_ref[...].T, axis=0, keepdims=True)
    tail_ref[:, 128:] = jnp.full((1, 128), jnp.sum(l_ref[...]), jnp.float32)

def pair(plan, f, t, s):
    n, v, blk = f.shape
    vp = -(-v//16)*16
    vm = pl.BlockSpec(memory_space=pltpu.VMEM)
    return pl.pallas_call(pair_kernel, in_specs=[pl.BlockSpec(memory_space=pltpu.SMEM), vm, vm, vm], out_specs=[vm]*2,
        out_shape=[jax.ShapeDtypeStruct((n,vp,blk),jnp.bfloat16), jax.ShapeDtypeStruct((1,256),jnp.float32)],
        scratch_shapes=[pltpu.VMEM((128,blk),jnp.float32), pltpu.VMEM((v,blk),jnp.float32)],
        compiler_params=pltpu.CompilerParams(vmem_limit_bytes=VMEM_SMALL), name="pair_terms")(plan,f,t,s)


def shards(latent, w_in, b_in, w_out, b_out, targets, var_weight, plan):
    hidden_in = latent[0]
    points, width = hidden_in.shape
    half = width // 2
    variables = w_out.shape[0]
    rounds, members = plan.shape
    member = lax.axis_index("member")
    grid_index = lax.axis_index("grid")
    grid_count = lax.axis_size("grid")
    devices = members * grid_count
    rows = w_in.shape[0]
    total = points * grid_count
    block = points // members
    core = lax.rem(grid_index, 2)
    swap = [(i, i ^ 1) for i in range(devices)]

    halves = jnp.stack([w_in[:, :half], w_in[:, half:]])
    send = jnp.broadcast_to(halves[None], (devices // 2, 2, rows, half))
    w_mine = lax.all_to_all(send.reshape(devices * rows, half), BOTH, 0, 0, tiled=True)
    w_other = lax.ppermute(w_mine, BOTH, swap)

    def part(a, which):
        return lax.dynamic_slice_in_dim(a, which * half, half, a.ndim - 1)

    tall = -(-variables // 8) * 8
    taller = -(-variables // 16) * 16
    out_pad = jnp.pad(w_out, ((0, taller - variables), (0, 0)))
    b_row = b_in[None, :]
    w_halves = (w_mine, w_other)
    b_halves = (part(b_row, core), part(b_row, 1 - core))
    o_halves = (part(out_pad, core), part(out_pad, 1 - core))

    bias = jnp.pad(b_out, (0, tall - variables))[:, None]
    partial = forward_half(
        True, hidden_in, w_mine, b_halves[0], o_halves[0], bias, tall, members
    )
    out = forward_half(
        False, hidden_in, w_other, b_halves[1], o_halves[1], partial, tall, members
    )

    fields = lax.all_to_all(out, "member", 0, 0, tiled=True)
    place = grid_index * points + member * block + jnp.arange(block, dtype=jnp.int32)
    area = jnp.cos(1.4 * (place.astype(jnp.float32) + 0.5) / total)
    scale_map = jnp.pad(area[None, :] * var_weight[:, None], ((0, tall - variables), (0, 0)))
    target = lax.dynamic_slice_in_dim(targets, member * block, block, 1)
    target = jnp.pad(target, ((0, tall - variables), (0, 0)))
    act1, g1 = slope_half(hidden_in, w_other, b_halves[1])
    act0, g0 = slope_half(hidden_in, w_mine, b_halves[0])
    fields, act1, g1 = lax.optimization_barrier((fields, act1, g1))
    cot, tail = pair(plan, fields, target, scale_map)
    back = lax.all_to_all(cot, "member", 0, 0, tiled=True)
    back, act0, g0 = lax.optimization_barrier((back, act0, g0))
    d1, pack1 = backward_half(
        back, o_halves[1], g1, hidden_in, act1, tail, variables, jnp.bfloat16
    )
    got = lax.ppermute(pack1, BOTH, swap)
    d0, pack0 = backward_half(
        back, o_halves[0], g0, hidden_in, act0, tail, variables, jnp.float32
    )
    mine = (pack0 + got.astype(jnp.float32)).astype(jnp.bfloat16)
    grad_hidden = sum(
        jnp.dot(d, w.T, preferred_element_type=jnp.float32) for d, w in zip((d0, d1), w_halves)
    ).astype(jnp.bfloat16)
    parts = lax.all_to_all(mine, BOTH, 0, 0, tiled=True)
    summed = jnp.sum(parts.reshape(devices // 2, 2, rows, -1).astype(jnp.float32), axis=0)
    own_rows = jnp.concatenate([summed[0, :, :half], summed[1, :, :half]], axis=1)
    small = jnp.concatenate([summed[0, :, half : half + 64], summed[1, :, half : half + 64]], axis=1)
    spread_small = jnp.broadcast_to(small[None], (devices,) + small.shape)
    everyone = lax.all_to_all(spread_small, BOTH, 0, 0)
    kappa = 4.0 / math.sqrt(members * total)
    grad_out, grad_bias, tails = finish(everyone, variables, width, kappa)
    tails = tails[0, :half] + tails[0, half:]
    loss = tails[128] / (members * total * variables)
    return (
        loss,
        grad_hidden[None],
        own_rows * kappa,
        grad_bias[0],
        grad_out,
        tails[:variables] * kappa,
    )


def solution(mesh):
    placed = (
        P("member", "grid", None),
        P(BOTH, None),
        P(),
        P(),
        P(),
        P(None, "grid"),
        P(),
        P(),
    )
    return jax.shard_map(
        shards,
        mesh=mesh,
        in_specs=placed,
        out_specs=(P(), P("member", "grid", None), P(BOTH, None), P(), P(), P()),
        check_vma=False,
    )
```

```python
import math

import jax
import jax.numpy as jnp
from jax import lax
from jax.experimental import pallas as pl
from jax.experimental.pallas import tpu as pltpu
from jax.sharding import PartitionSpec as P

DELTA = 0.25
BOTH = ("member", "grid")
VMEM_BYTES = 60 << 20
VMEM_SMALL = 24 << 20


GELU_A = 0.7978845608028654
GELU_B = 0.044715
WHOLE = pl.BlockSpec(memory_space=pltpu.VMEM)
HBM = pl.BlockSpec(memory_space=pltpu.HBM)


def shape(dims, kind):
    return jax.ShapeDtypeStruct(dims, kind)


def cost(flops, moved, special=0):
    return pl.CostEstimate(flops=flops, bytes_accessed=moved, transcendentals=special)


def load(src, dst, sem):
    copy = pltpu.make_async_copy(src, dst, sem)
    copy.start()
    return copy


def forward_kernel(first, parts, lat, w, b, o, extra, f_ref):
    points = lat.shape[0]
    half = w.shape[1]
    tile = points // parts
    rows, block = f_ref.shape[1:]
    for i in range(parts):
        sl = slice(i * tile, (i + 1) * tile)
        f = None
        for n in range(0, half, 256):
            cols = slice(n, n + 256)
            pre = jnp.dot(lat[sl, :], w[:, cols], preferred_element_type=jnp.float32) + b[:, cols]
            t = jnp.tanh(pre * (GELU_A + (GELU_A * GELU_B) * (pre * pre)))
            act = (pre * (0.5 + 0.5 * t)).astype(jnp.bfloat16)
            g = lax.dot_general(
                o[:, cols], act, (((1,), (1,)), ((), ())), preferred_element_type=jnp.float32
            )
            f = g if f is None else f + g
        for q in range(tile // block):
            at = i * (tile // block) + q
            piece = f[:rows, q * block : (q + 1) * block]
            f_ref[at] = piece + (extra[...] if first else extra[at])


def forward_half(first, lat, w, b, o, extra, rows, blocks):
    points, width = lat.shape
    half = w.shape[1]
    return pl.pallas_call(
        lambda *refs: forward_kernel(first, 4, *refs),
        in_specs=[WHOLE] * 5,
        out_specs=WHOLE,
        out_shape=shape((blocks, rows, points // blocks), jnp.float32),
        compiler_params=pltpu.CompilerParams(vmem_limit_bytes=VMEM_SMALL),
        cost_estimate=cost(2 * points * half * (width + rows), points * 2 * width, points * half),
        name="forward_half",
    )(lat, w, b, o, extra)


def slope_kernel(parts, lat_ref, w_ref, b, act_ref, g_ref, act_v, g_v, lat, w, sems, out_sems):
    points = lat.shape[0]
    half = w.shape[1]
    tile = points // parts
    slices = [slice(i * tile, (i + 1) * tile) for i in range(parts)]

    def fetch(i):
        return load(lat_ref.at[slices[i]], lat.at[slices[i]], sems.at[i])

    ready_w = load(w_ref, w, sems.at[parts])
    ready = [fetch(0)]
    ready_w.wait()
    out = []
    for i, sl in enumerate(slices):
        ready[i].wait()
        if i + 1 < parts:
            ready.append(fetch(i + 1))
        for n in range(0, half, 256):
            cols = slice(n, n + 256)
            pre = jnp.dot(lat[sl, :], w[:, cols], preferred_element_type=jnp.float32) + b[:, cols]
            sq = pre * pre
            t = jnp.tanh(pre * (GELU_A + (GELU_A * GELU_B) * sq))
            gate = 0.5 + 0.5 * t
            act_v[sl, cols] = (pre * gate).astype(jnp.bfloat16)
            inner = (0.5 * pre) * (1.0 - t * t) * (GELU_A + (3.0 * GELU_A * GELU_B) * sq)
            g_v[sl, cols] = (gate + inner).astype(jnp.bfloat16)
        out.append(load(act_v.at[sl], act_ref.at[sl], out_sems.at[2 * i]))
        out.append(load(g_v.at[sl], g_ref.at[sl], out_sems.at[2 * i + 1]))
    for copy in out:
        copy.wait()


def slope_half(lat, w, b):
    points, width = lat.shape
    half = w.shape[1]
    parts = 4
    return pl.pallas_call(
        lambda *refs: slope_kernel(parts, *refs),
        in_specs=[HBM] * 2 + [WHOLE],
        out_specs=[HBM] * 2,
        out_shape=[shape((points, half), jnp.bfloat16)] * 2,
        scratch_shapes=[
            pltpu.VMEM((points, half), jnp.bfloat16),
            pltpu.VMEM((points, half), jnp.bfloat16),
            pltpu.VMEM((points, width), jnp.bfloat16),
            pltpu.VMEM((width, half), jnp.bfloat16),
            pltpu.SemaphoreType.DMA((parts + 1,)),
            pltpu.SemaphoreType.DMA((2 * parts,)),
        ],
        compiler_params=pltpu.CompilerParams(vmem_limit_bytes=VMEM_BYTES),
        cost_estimate=cost(2 * points * half * width, points * (2 * width + 4 * half), points * half),
        name="slope_half",
    )(lat, w, b)


def cotangent_kernel(variables, parts, *refs):
    core, cot_ref = refs[:2]
    g_refs, act_refs = refs[2:4], refs[4:6]
    o_refs, tail = refs[6:8], refs[8]
    dpre_refs, pack_ref = refs[9:11], refs[11]
    cot, g, act, dpre_v, pack, table, sems, out_sems = refs[12:]
    blocks, rows, block = cot.shape
    points, half = g_refs[0].shape
    tile = points // parts
    steps = [(h, i) for h in range(2) for i in range(parts)]

    def fetch(n):
        h, i = steps[n]
        sl = slice(i * tile, (i + 1) * tile)
        return (
            load(g_refs[h].at[sl], g.at[h, sl], sems.at[1 + 2 * n]),
            load(act_refs[h].at[sl], act.at[h, sl], sems.at[2 + 2 * n]),
        )

    ready_cot = load(cot_ref, cot, sems.at[0])
    ready = [fetch(0), fetch(1), fetch(2)]
    ready_cot.wait()
    out = []
    for n, (h, i) in enumerate(steps):
        if i == 0:
            b1, w2 = None, None
        for copy in ready[n]:
            copy.wait()
        if n + 3 < len(steps):
            ready.append(fetch(n + 3))
        for q in range(i * blocks // parts, (i + 1) * blocks // parts):
            sl = slice(q * block, (q + 1) * block)
            dact = lax.dot_general(
                cot[q], o_refs[h][...], (((0,), (0,)), ((), ())), preferred_element_type=jnp.float32
            )
            dpre = dact * g[h, sl, :].astype(jnp.float32)
            dpre_v[h, sl, :] = dpre.astype(jnp.bfloat16)
            s = jnp.sum(dpre.reshape(-1, 8, half), axis=0)
            b1 = s if b1 is None else b1 + s
            a = jnp.dot(cot[q], act[h, sl, :], preferred_element_type=jnp.float32)
            w2 = a if w2 is None else w2 + a
        sl = slice(i * tile, (i + 1) * tile)
        out.append(load(dpre_v.at[h, sl], dpre_refs[h].at[sl], out_sems.at[n]))
        if i == parts - 1:
            table[h] = jnp.zeros(table.shape[1:], jnp.float32)
            table[h, :rows, :] = w2
            table[h, variables : variables + 1, :] = jnp.sum(b1, axis=0, keepdims=True)
            if h == 0:
                table[h, variables + 1 : variables + 2, : tail.shape[1]] = tail[...]
    lanes = half // 128
    low = core[0] == 0
    for unit in range(pack.shape[0] // 16):
        r, c = unit // lanes, unit % lanes
        pieces = []
        for h in range(2):
            piece = table[h, 8 * r : 8 * r + 8, 128 * c : 128 * (c + 1)]
            pieces.append(jnp.concatenate([piece[:, :64], piece[:, 64:]], axis=0))
        first = jnp.where(low, pieces[0], pieces[1])
        second = jnp.where(low, pieces[1], pieces[0])
        pack[16 * unit : 16 * unit + 16, :] = jnp.concatenate([first, second], axis=1).astype(jnp.bfloat16)
    out.append(load(pack, pack_ref, out_sems.at[len(steps)]))
    for copy in out:
        copy.wait()


def cotangents(core, cot, gs, acts, o_halves, tail, variables, width):
    points, half = gs[0].shape
    parts = 4
    row = shape((points, half), jnp.bfloat16)
    return pl.pallas_call(
        lambda *refs: cotangent_kernel(variables, parts, *refs),
        in_specs=[pl.BlockSpec(memory_space=pltpu.SMEM)] + [HBM] * 5 + [WHOLE] * 3,
        out_specs=[HBM] * 3,
        out_shape=[row, row, shape((width, 128), jnp.bfloat16)],
        scratch_shapes=[
            pltpu.VMEM(cot.shape, jnp.bfloat16),
            pltpu.VMEM((2, points, half), jnp.bfloat16),
            pltpu.VMEM((2, points, half), jnp.bfloat16),
            pltpu.VMEM((2, points, half), jnp.bfloat16),
            pltpu.VMEM((width, 128), jnp.bfloat16),
            pltpu.VMEM((2, width // 8, half), jnp.float32),
            pltpu.SemaphoreType.DMA((1 + 4 * parts,)),
            pltpu.SemaphoreType.DMA((1 + 2 * parts,)),
        ],
        compiler_params=pltpu.CompilerParams(vmem_limit_bytes=VMEM_BYTES),
        cost_estimate=cost(8 * points * half * cot.shape[1], points * 12 * half),
        name="cotangents",
    )(core, cot, *gs, *acts, *o_halves, tail)


def weight_kernel(parts, lat_ref, d_ref, out_ref, lat, d, total, sems, out_sems):
    width = lat.shape[1]
    cut = width // parts

    def fetch(i):
        cols = pl.ds(i * cut, cut)
        return load(lat_ref.at[:, cols], lat.at[:, cols], sems.at[i])

    ready_d = load(d_ref, d, sems.at[parts])
    ready = [fetch(0), fetch(1)]
    ready_d.wait()
    out = []
    for i in range(parts):
        ready[i].wait()
        if i + 2 < parts:
            ready.append(fetch(i + 2))
        sl = slice(i * cut, (i + 1) * cut)
        total[sl, :] = lax.dot_general(
            lat[:, sl], d[...], (((0,), (0,)), ((), ())), preferred_element_type=jnp.float32
        ).astype(total.dtype)
        out.append(load(total.at[sl], out_ref.at[sl], out_sems.at[i]))
    for copy in out:
        copy.wait()


def weight_half(lat, d, kind):
    points, half = d.shape
    width = lat.shape[1]
    parts = 4
    return pl.pallas_call(
        lambda *refs: weight_kernel(parts, *refs),
        in_specs=[HBM] * 2,
        out_specs=HBM,
        out_shape=shape((width, half), kind),
        scratch_shapes=[
            pltpu.VMEM(lat.shape, jnp.bfloat16),
            pltpu.VMEM(d.shape, jnp.bfloat16),
            pltpu.VMEM((width, half), kind),
            pltpu.SemaphoreType.DMA((parts + 1,)),
            pltpu.SemaphoreType.DMA((parts,)),
        ],
        compiler_params=pltpu.CompilerParams(vmem_limit_bytes=VMEM_BYTES),
        cost_estimate=cost(2 * points * half * width, points * 2 * (width + half) + width * half * 4),
        name="weight_half",
    )(lat, d)


def join_kernel(high, flag, table, mine, got, out_ref):
    rows, half = mine.shape
    acc = table[0:16, :].astype(jnp.float32)
    for u in range(1, rows // 16):
        acc = acc + table[16 * u : 16 * u + 16, :].astype(jnp.float32)
    small = acc[:8] + acc[8:]
    rest = small - small.astype(jnp.bfloat16).astype(jnp.float32)
    line = lax.broadcasted_iota(jnp.int32, small.shape, 0)
    low = jnp.broadcast_to(rest[high : high + 1], small.shape)
    small = jnp.where((line == high + 1) & (flag[0] == 1), low, small)
    both = jnp.concatenate([small, small], axis=0).astype(jnp.bfloat16)
    for u in range(rows // 16):
        sl = slice(16 * u, 16 * u + 16)
        out_ref[sl, :half] = (mine[sl, :] + got[sl, :].astype(jnp.float32)).astype(jnp.bfloat16)
        out_ref[sl, half:] = both


def join(flag, table, mine, got, high):
    rows, half = mine.shape
    return pl.pallas_call(
        lambda *refs: join_kernel(high, *refs),
        in_specs=[pl.BlockSpec(memory_space=pltpu.SMEM)] + [WHOLE] * 3,
        out_specs=WHOLE,
        out_shape=shape((rows, half + 128), jnp.bfloat16),
        compiler_params=pltpu.CompilerParams(vmem_limit_bytes=VMEM_SMALL),
        name="join",
    )(flag, table, mine, got)


def finish_kernel(kappa, share, all_ref, own_ref, w2_ref, b1_ref, b2_ref, loss_ref, tail):
    variables, width = w2_ref.shape
    half = width // 2
    lanes = half // 128
    acc = all_ref[0:16, :half].astype(jnp.float32)
    for u in range(1, all_ref.shape[0] // 16):
        acc = acc + all_ref[16 * u : 16 * u + 16, :half].astype(jnp.float32)
    own_ref[:, :half] = acc[:8] * kappa
    own_ref[:, half:] = acc[8:] * kappa
    for r in range(-(-(variables + 3) // 8)):
        for c in range(lanes):
            u = r * lanes + c
            pair_rows = all_ref[16 * u : 16 * u + 16, half:].astype(jnp.float32)
            a, b = pair_rows[:8], pair_rows[8:]
            for h in range(2):
                piece = jnp.concatenate([a[:, 64 * h : 64 * h + 64], b[:, 64 * h : 64 * h + 64]], axis=1)
                cols = slice(h * half + 128 * c, h * half + 128 * (c + 1))
                low = 8 * r
                keep = min(8, variables - low)
                if keep > 0:
                    w2_ref[low : low + keep, cols] = piece[:keep] * kappa
                at = variables - low
                if 0 <= at < 8:
                    b1_ref[:, cols] = piece[at : at + 1] * kappa
                    tail[:, cols] = piece[at + 1 : at + 2] + piece[at + 2 : at + 3]
    both = tail[:, :half] + tail[:, half:]
    b2_ref[...] = both[:, :128] * kappa
    loss_ref[...] = both[:, 128:256] * share


def finish(everyone, rows, variables, width, kappa, share):
    return pl.pallas_call(
        lambda *refs: finish_kernel(kappa, share, *refs),
        in_specs=[WHOLE],
        out_specs=[WHOLE] * 5,
        out_shape=[
            shape((rows, width), jnp.float32),
            shape((variables, width), jnp.float32),
            shape((1, width), jnp.float32),
            shape((1, 128), jnp.float32),
            shape((1, 128), jnp.float32),
        ],
        scratch_shapes=[pltpu.VMEM((1, width), jnp.float32)],
        compiler_params=pltpu.CompilerParams(vmem_limit_bytes=VMEM_SMALL),
        name="finish",
    )(everyone)


def pair_kernel(plan_ref, f_ref, t_ref, s_ref, cot_ref, tail_ref, b2_ref, l_ref):
    n, v, blk = f_ref.shape
    rounds = plan_ref.shape[0]
    vp = cot_ref.shape[1]
    D = DELTA
    b2_ref[...] = jnp.zeros_like(b2_ref); l_ref[...] = jnp.zeros_like(l_ref)
    cot_ref[...] = jnp.zeros_like(cot_ref)
    RB = 16
    def body(m, _):
        for r0 in range(0, v, RB):
            rs = slice(r0, min(r0+RB, v))
            f = f_ref[m, rs, :]
            sc = s_ref[rs, :]
            d = f - t_ref[rs, :]
            q = d*d + D*D
            inv = lax.rsqrt(q)
            slope = d*inv
            spread = q*inv - D
            ps = jnp.zeros_like(f); pr = jnp.zeros_like(f)
            for r in range(rounds):
                x = f - f_ref[plan_ref[r, m], rs, :]
                y = x*x + D*D
                iv = lax.rsqrt(y)
                ps += x*iv
                pr += y*iv - D
            cot = sc*(slope - ps*(1.0/rounds))
            b2_ref[rs, :] += cot
            l_ref[rs, :] += sc*(spread - pr*(0.5/rounds))
            h = min(RB, v-r0)
            cb = cot.astype(jnp.bfloat16)
            if h < RB:
                cb = jnp.concatenate([cb.astype(jnp.float32), jnp.zeros((RB-h, blk), jnp.float32)]).astype(jnp.bfloat16)
            cot_ref[m, r0:r0+RB, :] = cb
        return 0
    lax.fori_loop(0, n, body, 0)
    tail_ref[:, :128] = jnp.sum(b2_ref[...].T, axis=0, keepdims=True)
    tail_ref[:, 128:] = jnp.full((1, 128), jnp.sum(l_ref[...]), jnp.float32)

def pair(plan, f, t, s):
    n, v, blk = f.shape
    vp = -(-v//16)*16
    vm = pl.BlockSpec(memory_space=pltpu.VMEM)
    return pl.pallas_call(pair_kernel, in_specs=[pl.BlockSpec(memory_space=pltpu.SMEM), vm, vm, vm], out_specs=[vm]*2,
        out_shape=[jax.ShapeDtypeStruct((n,vp,blk),jnp.bfloat16), jax.ShapeDtypeStruct((1,256),jnp.float32)],
        scratch_shapes=[pltpu.VMEM((128,blk),jnp.float32), pltpu.VMEM((v,blk),jnp.float32)],
        compiler_params=pltpu.CompilerParams(vmem_limit_bytes=VMEM_SMALL), name="pair_terms")(plan,f,t,s)


def shards(latent, w_in, b_in, w_out, b_out, targets, var_weight, plan):
    hidden_in = latent[0]
    points, width = hidden_in.shape
    half = width // 2
    variables = w_out.shape[0]
    rounds, members = plan.shape
    member = lax.axis_index("member")
    grid_index = lax.axis_index("grid")
    grid_count = lax.axis_size("grid")
    devices = members * grid_count
    rows = w_in.shape[0]
    total = points * grid_count
    block = points // members
    core = lax.rem(grid_index, 2)
    swap = [(i, i ^ 1) for i in range(devices)]

    halves = jnp.stack([w_in[:, :half], w_in[:, half:]])
    send = jnp.broadcast_to(halves[None], (devices // 2, 2, rows, half))
    w_mine = lax.all_to_all(send.reshape(devices * rows, half), BOTH, 0, 0, tiled=True)
    w_other = lax.ppermute(w_mine, BOTH, swap)

    def part(a, which):
        return lax.dynamic_slice_in_dim(a, which * half, half, a.ndim - 1)

    tall = -(-variables // 8) * 8
    taller = -(-variables // 16) * 16
    out_pad = jnp.pad(w_out, ((0, taller - variables), (0, 0)))
    b_row = b_in[None, :]
    w_halves = (w_mine, w_other)
    b_halves = (part(b_row, core), part(b_row, 1 - core))
    o_halves = (part(out_pad, core), part(out_pad, 1 - core))

    bias = jnp.pad(b_out, (0, tall - variables))[:, None]
    partial = forward_half(
        True, hidden_in, w_mine, b_halves[0], o_halves[0], bias, tall, members
    )
    out = forward_half(
        False, hidden_in, w_other, b_halves[1], o_halves[1], partial, tall, members
    )

    fields = lax.all_to_all(out, "member", 0, 0, tiled=True)
    place = grid_index * points + member * block + jnp.arange(block, dtype=jnp.int32)
    area = jnp.cos(1.4 * (place.astype(jnp.float32) + 0.5) / total)
    scale_map = jnp.pad(area[None, :] * var_weight[:, None], ((0, tall - variables), (0, 0)))
    target = lax.dynamic_slice_in_dim(targets, member * block, block, 1)
    target = jnp.pad(target, ((0, tall - variables), (0, 0)))
    act1, g1 = slope_half(hidden_in, w_other, b_halves[1])
    act0, g0 = slope_half(hidden_in, w_mine, b_halves[0])
    fields, act1, g1 = lax.optimization_barrier((fields, act1, g1))
    cot, tail = pair(plan, fields, target, scale_map)
    back = lax.all_to_all(cot, "member", 0, 0, tiled=True)
    back, act0, g0 = lax.optimization_barrier((back, act0, g0))
    place = member * grid_count + grid_index
    tail_row = variables + 1
    flag = (place // 8 == tail_row // 8).astype(jnp.int32)[None]
    d0, d1, pack = cotangents(
        core[None], back, (g0, g1), (act0, act1), o_halves, tail, variables, width
    )
    tables = lax.all_to_all(pack, BOTH, 0, 0, tiled=True)
    got = lax.ppermute(weight_half(hidden_in, d1, jnp.bfloat16), BOTH, swap)
    mine = weight_half(hidden_in, d0, jnp.float32)
    chunks = join(flag, tables, mine, got, tail_row % 8)
    chunks, d0, d1 = lax.optimization_barrier((chunks, d0, d1))
    parts = lax.all_to_all(chunks, BOTH, 0, 0, tiled=True)
    grad_hidden = sum(
        jnp.dot(d, w.T, preferred_element_type=jnp.float32) for d, w in zip((d0, d1), w_halves)
    ).astype(jnp.bfloat16)
    kappa = 4.0 / math.sqrt(members * total)
    own_rows, grad_out, grad_bias, grad_b_out, loss = finish(
        parts, rows, variables, width, kappa, 1.0 / (members * total * variables)
    )
    return (
        loss[0, 0],
        grad_hidden[None],
        own_rows,
        grad_bias[0],
        grad_out,
        grad_b_out[0, :variables],
    )


def solution(mesh):
    placed = (
        P("member", "grid", None),
        P(BOTH, None),
        P(),
        P(),
        P(),
        P(None, "grid"),
        P(),
        P(),
    )
    return jax.shard_map(
        shards,
        mesh=mesh,
        in_specs=placed,
        out_specs=(P(), P("member", "grid", None), P(BOTH, None), P(), P(), P()),
        check_vma=False,
    )
```

```python
import math

import jax
import jax.numpy as jnp
from jax import lax
from jax.experimental import pallas as pl
from jax.experimental.pallas import tpu as pltpu
from jax.sharding import PartitionSpec as P

DELTA = 0.25
BOTH = ("member", "grid")
VMEM_BYTES = 60 << 20
VMEM_SMALL = 24 << 20


GELU_A = 0.7978845608028654
GELU_B = 0.044715
WHOLE = pl.BlockSpec(memory_space=pltpu.VMEM)
HBM = pl.BlockSpec(memory_space=pltpu.HBM)
ANY = pl.BlockSpec(memory_space=pl.ANY)


def shape(dims, kind):
    return jax.ShapeDtypeStruct(dims, kind)


def cost(flops, moved, special=0):
    return pl.CostEstimate(flops=flops, bytes_accessed=moved, transcendentals=special)


def load(src, dst, sem):
    copy = pltpu.make_async_copy(src, dst, sem)
    copy.start()
    return copy


def forward_kernel(first, parts, lat, w, b, o, extra, f_ref):
    points = lat.shape[0]
    half = w.shape[1]
    tile = points // parts
    rows, block = f_ref.shape[1:]
    for i in range(parts):
        sl = slice(i * tile, (i + 1) * tile)
        f = None
        for n in range(0, half, 256):
            cols = slice(n, n + 256)
            pre = jnp.dot(lat[sl, :], w[:, cols], preferred_element_type=jnp.float32) + b[:, cols]
            t = jnp.tanh(pre * (GELU_A + (GELU_A * GELU_B) * (pre * pre)))
            act = (pre * (0.5 + 0.5 * t)).astype(jnp.bfloat16)
            g = lax.dot_general(
                o[:, cols], act, (((1,), (1,)), ((), ())), preferred_element_type=jnp.float32
            )
            f = g if f is None else f + g
        for q in range(tile // block):
            at = i * (tile // block) + q
            piece = f[:rows, q * block : (q + 1) * block]
            f_ref[at] = piece + (extra[...] if first else extra[at])


def forward_half(first, lat, w, b, o, extra, rows, blocks):
    points, width = lat.shape
    half = w.shape[1]
    return pl.pallas_call(
        lambda *refs: forward_kernel(first, 2, *refs),
        in_specs=[WHOLE] * 5,
        out_specs=WHOLE,
        out_shape=shape((blocks, rows, points // blocks), jnp.float32),
        compiler_params=pltpu.CompilerParams(vmem_limit_bytes=VMEM_SMALL),
        cost_estimate=cost(2 * points * half * (width + rows), points * 2 * width, points * half),
        name="forward_half",
    )(lat, w, b, o, extra)


def slope_kernel(parts, lat_ref, w_ref, b, act_ref, g_ref, act_v, g_v, lat, w, sems, out_sems):
    points = lat.shape[0]
    half = w.shape[1]
    tile = points // parts
    slices = [slice(i * tile, (i + 1) * tile) for i in range(parts)]

    def fetch(i):
        return load(lat_ref.at[slices[i]], lat.at[slices[i]], sems.at[i])

    ready_w = load(w_ref, w, sems.at[parts])
    ready = [fetch(i) for i in range(parts)]
    ready_w.wait()
    out = []
    for i, sl in enumerate(slices):
        ready[i].wait()
        for n in range(0, half, 256):
            cols = slice(n, n + 256)
            pre = jnp.dot(lat[sl, :], w[:, cols], preferred_element_type=jnp.float32) + b[:, cols]
            sq = pre * pre
            t = jnp.tanh(pre * (GELU_A + (GELU_A * GELU_B) * sq))
            gate = 0.5 + 0.5 * t
            act_v[sl, cols] = (pre * gate).astype(jnp.bfloat16)
            inner = (0.5 * pre) * (1.0 - t * t) * (GELU_A + (3.0 * GELU_A * GELU_B) * sq)
            g_v[sl, cols] = (gate + inner).astype(jnp.bfloat16)
        out.append(load(act_v.at[sl], act_ref.at[sl], out_sems.at[2 * i]))
        out.append(load(g_v.at[sl], g_ref.at[sl], out_sems.at[2 * i + 1]))
    for copy in out:
        copy.wait()


def slope_half(lat, w, b):
    points, width = lat.shape
    half = w.shape[1]
    parts = 4
    return pl.pallas_call(
        lambda *refs: slope_kernel(parts, *refs),
        in_specs=[HBM] * 2 + [WHOLE],
        out_specs=[HBM] * 2,
        out_shape=[shape((points, half), jnp.bfloat16)] * 2,
        scratch_shapes=[
            pltpu.VMEM((points, half), jnp.bfloat16),
            pltpu.VMEM((points, half), jnp.bfloat16),
            pltpu.VMEM((points, width), jnp.bfloat16),
            pltpu.VMEM((width, half), jnp.bfloat16),
            pltpu.SemaphoreType.DMA((parts + 1,)),
            pltpu.SemaphoreType.DMA((2 * parts,)),
        ],
        compiler_params=pltpu.CompilerParams(vmem_limit_bytes=VMEM_BYTES),
        cost_estimate=cost(2 * points * half * width, points * (2 * width + 4 * half), points * half),
        name="slope_half",
    )(lat, w, b)


def cotangent_kernel(variables, parts, *refs):
    core, cot_ref = refs[:2]
    g_refs, act_refs, lat_ref = refs[2:4], refs[4:6], refs[6]
    o_refs, tail = refs[7:9], refs[9]
    dpre_refs, pack_ref, give_ref = refs[10:12], refs[12], refs[13]
    cot, g, act, dpre_v, pack, table, lat, give, sems, lat_sem, out_sems, give_sems = refs[14:]
    blocks, rows, block = cot.shape
    points, half = g_refs[0].shape
    tile = points // parts
    steps = [(h, i) for h in range(2) for i in range(parts)]

    def fetch(n):
        h, i = steps[n]
        sl = slice(i * tile, (i + 1) * tile)
        return (
            load(g_refs[h].at[sl], g.at[h, sl], sems.at[1 + 2 * n]),
            load(act_refs[h].at[sl], act.at[h, sl], sems.at[2 + 2 * n]),
        )

    ready_cot = load(cot_ref, cot, sems.at[0])
    ready = [fetch(n) for n in range(len(steps))]
    ready_lat = load(lat_ref, lat, lat_sem)
    ready_cot.wait()
    out = []
    for n, (h, i) in enumerate(steps):
        if i == 0:
            b1, w2 = None, None
        for copy in ready[n]:
            copy.wait()
        for q in range(i * blocks // parts, (i + 1) * blocks // parts):
            sl = slice(q * block, (q + 1) * block)
            dact = lax.dot_general(
                cot[q], o_refs[h][...], (((0,), (0,)), ((), ())), preferred_element_type=jnp.float32
            )
            dpre = dact * g[h, sl, :].astype(jnp.float32)
            dpre_v[h, sl, :] = dpre.astype(jnp.bfloat16)
            s = jnp.sum(dpre.reshape(-1, 8, half), axis=0)
            b1 = s if b1 is None else b1 + s
            a = jnp.dot(cot[q], act[h, sl, :], preferred_element_type=jnp.float32)
            w2 = a if w2 is None else w2 + a
        sl = slice(i * tile, (i + 1) * tile)
        out.append(load(dpre_v.at[h, sl], dpre_refs[h].at[sl], out_sems.at[n]))
        if i == parts - 1:
            table[h] = jnp.zeros(table.shape[1:], jnp.float32)
            table[h, :rows, :] = w2
            table[h, variables : variables + 1, :] = jnp.sum(b1, axis=0, keepdims=True)
            if h == 0:
                table[h, variables + 1 : variables + 2, : tail.shape[1]] = tail[...]
    lanes = half // 128
    low = core[0] == 0
    for unit in range(pack.shape[0] // 16):
        r, c = unit // lanes, unit % lanes
        pieces = []
        for h in range(2):
            piece = table[h, 8 * r : 8 * r + 8, 128 * c : 128 * (c + 1)]
            pieces.append(jnp.concatenate([piece[:, :64], piece[:, 64:]], axis=0))
        first = jnp.where(low, pieces[0], pieces[1])
        second = jnp.where(low, pieces[1], pieces[0])
        pack[16 * unit : 16 * unit + 16, :] = jnp.concatenate([first, second], axis=1).astype(jnp.bfloat16)
    out.append(load(pack, pack_ref, out_sems.at[len(steps)]))
    ready_lat.wait()
    cut = lat.shape[1] // parts
    for m in range(parts):
        at = slice(m * cut, (m + 1) * cut)
        give[at, :] = lax.dot_general(
            lat[:, at], dpre_v[1], (((0,), (0,)), ((), ())), preferred_element_type=jnp.float32
        ).astype(jnp.bfloat16)
        out.append(load(give.at[at], give_ref.at[at], give_sems.at[m]))
    for copy in out:
        copy.wait()


def cotangents(core, cot, gs, acts, lat, o_halves, tail, variables):
    width = lat.shape[1]
    points, half = gs[0].shape
    parts = 4
    row = shape((points, half), jnp.bfloat16)
    return pl.pallas_call(
        lambda *refs: cotangent_kernel(variables, parts, *refs),
        in_specs=[pl.BlockSpec(memory_space=pltpu.SMEM), ANY] + [HBM] * 5 + [WHOLE] * 3,
        out_specs=[HBM] * 4,
        out_shape=[row, row, shape((width, 128), jnp.bfloat16), shape((width, half), jnp.bfloat16)],
        scratch_shapes=[
            pltpu.VMEM(cot.shape, jnp.bfloat16),
            pltpu.VMEM((2, points, half), jnp.bfloat16),
            pltpu.VMEM((2, points, half), jnp.bfloat16),
            pltpu.VMEM((2, points, half), jnp.bfloat16),
            pltpu.VMEM((width, 128), jnp.bfloat16),
            pltpu.VMEM((2, width // 8, half), jnp.float32),
            pltpu.VMEM(lat.shape, jnp.bfloat16),
            pltpu.VMEM((width, half), jnp.bfloat16),
            pltpu.SemaphoreType.DMA((1 + 4 * parts,)),
            pltpu.SemaphoreType.DMA,
            pltpu.SemaphoreType.DMA((1 + 2 * parts,)),
            pltpu.SemaphoreType.DMA((parts,)),
        ],
        compiler_params=pltpu.CompilerParams(vmem_limit_bytes=VMEM_BYTES),
        cost_estimate=cost(2 * points * half * (4 * cot.shape[1] + width), points * (12 * half + 2 * width)),
        name="cotangents",
    )(core, cot, *gs, *acts, lat, *o_halves, tail)


def weight_kernel(parts, fused, *refs):
    lat_ref, d_ref = refs[:2]
    got_ref = refs[2] if fused else None
    out_ref, lat, d, acc, total, sems, out_sems = refs[2 + fused :][:7]
    width = lat.shape[1]
    points, half = d.shape
    tile = points // parts
    cut = width // parts
    ready = []
    for i in range(parts):
        sl = slice(i * tile, (i + 1) * tile)
        ready.append((load(d_ref.at[sl], d.at[sl], sems.at[2 * i]), load(lat_ref.at[sl], lat.at[sl], sems.at[2 * i + 1])))
    if fused:
        got = refs[-1]
        ready_got = load(got_ref, got, sems.at[2 * parts])
    out = []
    for i in range(parts):
        for copy in ready[i]:
            copy.wait()
        if fused and i == parts - 1:
            ready_got.wait()
        sl = slice(i * tile, (i + 1) * tile)
        for m in range(parts):
            at = slice(m * cut, (m + 1) * cut)
            term = lax.dot_general(
                lat[sl, at], d[sl, :], (((0,), (0,)), ((), ())), preferred_element_type=jnp.float32
            )
            if i > 0:
                term = term + acc[at, :]
            if i < parts - 1:
                acc[at, :] = term
                continue
            if fused:
                term = term + got[at, :].astype(jnp.float32)
            total[at, :] = term.astype(jnp.bfloat16)
            out.append(load(total.at[at], out_ref.at[at], out_sems.at[m]))
    for copy in out:
        copy.wait()


def weight_half(lat, d, *got):
    points, half = d.shape
    width = lat.shape[1]
    parts = 4
    fused = len(got)
    small = pltpu.VMEM((width, half), jnp.bfloat16)
    return pl.pallas_call(
        lambda *refs: weight_kernel(parts, fused, *refs),
        in_specs=[HBM] * 2 + [ANY] * fused,
        out_specs=ANY,
        out_shape=shape((width, half), jnp.bfloat16),
        scratch_shapes=[
            pltpu.VMEM(lat.shape, jnp.bfloat16),
            pltpu.VMEM(d.shape, jnp.bfloat16),
            pltpu.VMEM((width, half), jnp.float32),
            small,
            pltpu.SemaphoreType.DMA((2 * parts + 1,)),
            pltpu.SemaphoreType.DMA((parts,)),
        ]
        + [small] * fused,
        compiler_params=pltpu.CompilerParams(vmem_limit_bytes=VMEM_BYTES),
        cost_estimate=cost(2 * points * half * width, points * 2 * (width + half) + width * half * 4),
        name="weight_half",
    )(lat, d, *got)


def join_kernel(high, flag, table, mine, out_ref):
    rows, half = mine.shape
    acc = table[0:16, :].astype(jnp.float32)
    for u in range(1, rows // 16):
        acc = acc + table[16 * u : 16 * u + 16, :].astype(jnp.float32)
    small = acc[:8] + acc[8:]
    rest = small - small.astype(jnp.bfloat16).astype(jnp.float32)
    line = lax.broadcasted_iota(jnp.int32, small.shape, 0)
    low = jnp.broadcast_to(rest[high : high + 1], small.shape)
    small = jnp.where((line == high + 1) & (flag[0] == 1), low, small)
    both = jnp.concatenate([small, small], axis=0).astype(jnp.bfloat16)
    for u in range(rows // 16):
        sl = slice(16 * u, 16 * u + 16)
        out_ref[sl, :half] = mine[sl, :]
        out_ref[sl, half:] = both


def join(flag, table, mine, high):
    rows, half = mine.shape
    return pl.pallas_call(
        lambda *refs: join_kernel(high, *refs),
        in_specs=[pl.BlockSpec(memory_space=pltpu.SMEM)] + [WHOLE] * 2,
        out_specs=WHOLE,
        out_shape=shape((rows, half + 128), jnp.bfloat16),
        compiler_params=pltpu.CompilerParams(vmem_limit_bytes=VMEM_SMALL),
        name="join",
    )(flag, table, mine)


def finish_kernel(kappa, share, all_ref, own_ref, w2_ref, b1_ref, b2_ref, loss_ref, tail):
    variables, width = w2_ref.shape
    half = width // 2
    lanes = half // 128
    acc = all_ref[0:16, :half].astype(jnp.float32)
    for u in range(1, all_ref.shape[0] // 16):
        acc = acc + all_ref[16 * u : 16 * u + 16, :half].astype(jnp.float32)
    own_ref[:, :half] = acc[:8] * kappa
    own_ref[:, half:] = acc[8:] * kappa
    for r in range(-(-(variables + 3) // 8)):
        for c in range(lanes):
            u = r * lanes + c
            pair_rows = all_ref[16 * u : 16 * u + 16, half:].astype(jnp.float32)
            a, b = pair_rows[:8], pair_rows[8:]
            for h in range(2):
                piece = jnp.concatenate([a[:, 64 * h : 64 * h + 64], b[:, 64 * h : 64 * h + 64]], axis=1)
                cols = slice(h * half + 128 * c, h * half + 128 * (c + 1))
                low = 8 * r
                keep = min(8, variables - low)
                if keep > 0:
                    w2_ref[low : low + keep, cols] = piece[:keep] * kappa
                at = variables - low
                if 0 <= at < 8:
                    b1_ref[:, cols] = piece[at : at + 1] * kappa
                    tail[:, cols] = piece[at + 1 : at + 2] + piece[at + 2 : at + 3]
    both = tail[:, :half] + tail[:, half:]
    b2_ref[...] = both[:, :128] * kappa
    loss_ref[...] = both[:, 128:256] * share


def finish(everyone, rows, variables, width, kappa, share):
    return pl.pallas_call(
        lambda *refs: finish_kernel(kappa, share, *refs),
        in_specs=[WHOLE],
        out_specs=[WHOLE] * 5,
        out_shape=[
            shape((rows, width), jnp.float32),
            shape((variables, width), jnp.float32),
            shape((1, width), jnp.float32),
            shape((1, 128), jnp.float32),
            shape((1, 128), jnp.float32),
        ],
        scratch_shapes=[pltpu.VMEM((1, width), jnp.float32)],
        compiler_params=pltpu.CompilerParams(vmem_limit_bytes=VMEM_SMALL),
        name="finish",
    )(everyone)


def pair_kernel(plan_ref, f_ref, t_ref, s_ref, cot_ref, tail_ref, b2_ref, l_ref):
    n, v, blk = f_ref.shape
    rounds = plan_ref.shape[0]
    vp = cot_ref.shape[1]
    D = DELTA
    b2_ref[...] = jnp.zeros_like(b2_ref); l_ref[...] = jnp.zeros_like(l_ref)
    cot_ref[...] = jnp.zeros_like(cot_ref)
    RB = 16
    def body(m, _):
        for r0 in range(0, v, RB):
            rs = slice(r0, min(r0+RB, v))
            f = f_ref[m, rs, :]
            sc = s_ref[rs, :]
            d = f - t_ref[rs, :]
            q = d*d + D*D
            inv = lax.rsqrt(q)
            slope = d*inv
            spread = q*inv - D
            ps = jnp.zeros_like(f); pr = jnp.zeros_like(f)
            for r in range(rounds):
                x = f - f_ref[plan_ref[r, m], rs, :]
                y = x*x + D*D
                iv = lax.rsqrt(y)
                ps += x*iv
                pr += y*iv - D
            cot = sc*(slope - ps*(1.0/rounds))
            b2_ref[rs, :] += cot
            l_ref[rs, :] += sc*(spread - pr*(0.5/rounds))
            h = min(RB, v-r0)
            cb = cot.astype(jnp.bfloat16)
            if h < RB:
                cb = jnp.concatenate([cb.astype(jnp.float32), jnp.zeros((RB-h, blk), jnp.float32)]).astype(jnp.bfloat16)
            cot_ref[m, r0:r0+RB, :] = cb
        return 0
    lax.fori_loop(0, n, body, 0)
    tail_ref[:, :128] = jnp.sum(b2_ref[...].T, axis=0, keepdims=True)
    tail_ref[:, 128:] = jnp.full((1, 128), jnp.sum(l_ref[...]), jnp.float32)

def pair(plan, f, t, s):
    n, v, blk = f.shape
    vp = -(-v//16)*16
    vm = pl.BlockSpec(memory_space=pltpu.VMEM)
    return pl.pallas_call(pair_kernel, in_specs=[pl.BlockSpec(memory_space=pltpu.SMEM), vm, vm, vm], out_specs=[vm]*2,
        out_shape=[jax.ShapeDtypeStruct((n,vp,blk),jnp.bfloat16), jax.ShapeDtypeStruct((1,256),jnp.float32)],
        scratch_shapes=[pltpu.VMEM((128,blk),jnp.float32), pltpu.VMEM((v,blk),jnp.float32)],
        compiler_params=pltpu.CompilerParams(vmem_limit_bytes=VMEM_SMALL), name="pair_terms")(plan,f,t,s)


def shards(latent, w_in, b_in, w_out, b_out, targets, var_weight, plan):
    hidden_in = latent[0]
    points, width = hidden_in.shape
    half = width // 2
    variables = w_out.shape[0]
    rounds, members = plan.shape
    member = lax.axis_index("member")
    grid_index = lax.axis_index("grid")
    grid_count = lax.axis_size("grid")
    devices = members * grid_count
    rows = w_in.shape[0]
    total = points * grid_count
    block = points // members
    core = lax.rem(grid_index, 2)
    swap = [(i, i ^ 1) for i in range(devices)]

    halves = jnp.stack([w_in[:, :half], w_in[:, half:]])
    send = jnp.broadcast_to(halves[None], (devices // 2, 2, rows, half))
    w_mine = lax.all_to_all(send.reshape(devices * rows, half), BOTH, 0, 0, tiled=True)
    w_other = lax.ppermute(w_mine, BOTH, swap)

    def part(a, which):
        return lax.dynamic_slice_in_dim(a, which * half, half, a.ndim - 1)

    tall = -(-variables // 8) * 8
    taller = -(-variables // 16) * 16
    out_pad = jnp.pad(w_out, ((0, taller - variables), (0, 0)))
    b_row = b_in[None, :]
    w_halves = (w_mine, w_other)
    b_halves = (part(b_row, core), part(b_row, 1 - core))
    o_halves = (part(out_pad, core), part(out_pad, 1 - core))

    bias = jnp.pad(b_out, (0, tall - variables))[:, None]
    partial = forward_half(
        True, hidden_in, w_mine, b_halves[0], o_halves[0], bias, tall, members
    )
    out = forward_half(
        False, hidden_in, w_other, b_halves[1], o_halves[1], partial, tall, members
    )

    fields = lax.all_to_all(out, "member", 0, 0, tiled=True)
    place = grid_index * points + member * block + jnp.arange(block, dtype=jnp.int32)
    area = jnp.cos(1.4 * (place.astype(jnp.float32) + 0.5) / total)
    scale_map = jnp.pad(area[None, :] * var_weight[:, None], ((0, tall - variables), (0, 0)))
    target = lax.dynamic_slice_in_dim(targets, member * block, block, 1)
    target = jnp.pad(target, ((0, tall - variables), (0, 0)))
    act1, g1 = slope_half(hidden_in, w_other, b_halves[1])
    act0, g0 = slope_half(hidden_in, w_mine, b_halves[0])
    fields, act1, g1 = lax.optimization_barrier((fields, act1, g1))
    cot, tail = pair(plan, fields, target, scale_map)
    back = lax.all_to_all(cot, "member", 0, 0, tiled=True)
    back, act0, g0 = lax.optimization_barrier((back, act0, g0))
    place = member * grid_count + grid_index
    tail_row = variables + 1
    flag = (place // 8 == tail_row // 8).astype(jnp.int32)[None]
    d0, d1, pack, give = cotangents(
        core[None], back, (g0, g1), (act0, act1), hidden_in, o_halves, tail, variables
    )
    tables = lax.all_to_all(pack, BOTH, 0, 0, tiled=True)
    got = lax.ppermute(give, BOTH, swap)
    mine = weight_half(hidden_in, d0, got)
    chunks = join(flag, tables, mine, tail_row % 8)
    chunks, d0, d1 = lax.optimization_barrier((chunks, d0, d1))
    parts = lax.all_to_all(chunks, BOTH, 0, 0, tiled=True)
    grad_hidden = sum(
        jnp.dot(d, w.T, preferred_element_type=jnp.float32) for d, w in zip((d0, d1), w_halves)
    ).astype(jnp.bfloat16)
    kappa = 4.0 / math.sqrt(members * total)
    own_rows, grad_out, grad_bias, grad_b_out, loss = finish(
        parts, rows, variables, width, kappa, 1.0 / (members * total * variables)
    )
    return (
        loss[0, 0],
        grad_hidden[None],
        own_rows,
        grad_bias[0],
        grad_out,
        grad_b_out[0, :variables],
    )


def solution(mesh):
    placed = (
        P("member", "grid", None),
        P(BOTH, None),
        P(),
        P(),
        P(),
        P(None, "grid"),
        P(),
        P(),
    )
    return jax.shard_map(
        shards,
        mesh=mesh,
        in_specs=placed,
        out_specs=(P(), P("member", "grid", None), P(BOTH, None), P(), P(), P()),
        check_vma=False,
    )
```

```python
import math

import jax
import jax.numpy as jnp
from jax import lax
from jax.experimental import pallas as pl
from jax.experimental.pallas import tpu as pltpu
from jax.sharding import PartitionSpec as P

DELTA = 0.25
BOTH = ("member", "grid")
VMEM_BYTES = 60 << 20
VMEM_SMALL = 24 << 20


GELU_A = 0.7978845608028654
GELU_B = 0.044715
WHOLE = pl.BlockSpec(memory_space=pltpu.VMEM)
HBM = pl.BlockSpec(memory_space=pltpu.HBM)
ANY = pl.BlockSpec(memory_space=pl.ANY)


def shape(dims, kind):
    return jax.ShapeDtypeStruct(dims, kind)


def cost(flops, moved, special=0):
    return pl.CostEstimate(flops=flops, bytes_accessed=moved, transcendentals=special)


def load(src, dst, sem):
    copy = pltpu.make_async_copy(src, dst, sem)
    copy.start()
    return copy


def forward_kernel(first, parts, lat, w, b, o, extra, f_ref):
    points = lat.shape[0]
    half = w.shape[1]
    tile = points // parts
    rows, block = f_ref.shape[1:]
    for i in range(parts):
        sl = slice(i * tile, (i + 1) * tile)
        f = None
        for n in range(0, half, 256):
            cols = slice(n, n + 256)
            pre = jnp.dot(lat[sl, :], w[:, cols], preferred_element_type=jnp.float32) + b[:, cols]
            t = jnp.tanh(pre * (GELU_A + (GELU_A * GELU_B) * (pre * pre)))
            act = (pre * (0.5 + 0.5 * t)).astype(jnp.bfloat16)
            g = lax.dot_general(
                o[:, cols], act, (((1,), (1,)), ((), ())), preferred_element_type=jnp.float32
            )
            f = g if f is None else f + g
        for q in range(tile // block):
            at = i * (tile // block) + q
            piece = f[:rows, q * block : (q + 1) * block]
            f_ref[at] = piece + (extra[...] if first else extra[at])


def forward_half(first, lat, w, b, o, extra, rows, blocks):
    points, width = lat.shape
    half = w.shape[1]
    return pl.pallas_call(
        lambda *refs: forward_kernel(first, 2, *refs),
        in_specs=[WHOLE] * 5,
        out_specs=WHOLE,
        out_shape=shape((blocks, rows, points // blocks), jnp.float32),
        compiler_params=pltpu.CompilerParams(vmem_limit_bytes=VMEM_SMALL),
        cost_estimate=cost(2 * points * half * (width + rows), points * 2 * width, points * half),
        name="forward_half",
    )(lat, w, b, o, extra)


def slope_kernel(parts, lat_ref, w_ref, b, act_ref, g_ref, act_v, g_v, lat, w, sems, out_sems):
    points = lat.shape[0]
    half = w.shape[1]
    tile = points // parts
    slices = [slice(i * tile, (i + 1) * tile) for i in range(parts)]

    def fetch(i):
        return load(lat_ref.at[slices[i]], lat.at[slices[i]], sems.at[i])

    ready_w = load(w_ref, w, sems.at[parts])
    ready = [fetch(i) for i in range(parts)]
    ready_w.wait()
    out = []
    for i, sl in enumerate(slices):
        ready[i].wait()
        for n in range(0, half, 256):
            cols = slice(n, n + 256)
            pre = jnp.dot(lat[sl, :], w[:, cols], preferred_element_type=jnp.float32) + b[:, cols]
            sq = pre * pre
            t = jnp.tanh(pre * (GELU_A + (GELU_A * GELU_B) * sq))
            gate = 0.5 + 0.5 * t
            act_v[sl, cols] = (pre * gate).astype(jnp.bfloat16)
            inner = (0.5 * pre) * (1.0 - t * t) * (GELU_A + (3.0 * GELU_A * GELU_B) * sq)
            g_v[sl, cols] = (gate + inner).astype(jnp.bfloat16)
        out.append(load(act_v.at[sl], act_ref.at[sl], out_sems.at[2 * i]))
        out.append(load(g_v.at[sl], g_ref.at[sl], out_sems.at[2 * i + 1]))
    for copy in out:
        copy.wait()


def slope_half(lat, w, b):
    points, width = lat.shape
    half = w.shape[1]
    parts = 4
    return pl.pallas_call(
        lambda *refs: slope_kernel(parts, *refs),
        in_specs=[HBM] * 2 + [WHOLE],
        out_specs=[HBM] * 2,
        out_shape=[shape((points, half), jnp.bfloat16)] * 2,
        scratch_shapes=[
            pltpu.VMEM((points, half), jnp.bfloat16),
            pltpu.VMEM((points, half), jnp.bfloat16),
            pltpu.VMEM((points, width), jnp.bfloat16),
            pltpu.VMEM((width, half), jnp.bfloat16),
            pltpu.SemaphoreType.DMA((parts + 1,)),
            pltpu.SemaphoreType.DMA((2 * parts,)),
        ],
        compiler_params=pltpu.CompilerParams(vmem_limit_bytes=VMEM_BYTES),
        cost_estimate=cost(2 * points * half * width, points * (2 * width + 4 * half), points * half),
        name="slope_half",
    )(lat, w, b)


def cotangent_kernel(variables, parts, *refs):
    core, cot_ref = refs[:2]
    g_refs, act_refs, lat_ref = refs[2:4], refs[4:6], refs[6]
    o_refs, tail = refs[7:9], refs[9]
    dpre_refs, pack_ref, give_ref = refs[10:12], refs[12], refs[13]
    cot, g, act, dpre_v, pack, table, lat, give, sems, lat_sem, out_sems, give_sems = refs[14:]
    blocks, rows, block = cot.shape
    points, half = g_refs[0].shape
    tile = points // parts
    steps = [(h, i) for h in range(2) for i in range(parts)]

    def fetch(n):
        h, i = steps[n]
        sl = slice(i * tile, (i + 1) * tile)
        return (
            load(g_refs[h].at[sl], g.at[h, sl], sems.at[1 + 2 * n]),
            load(act_refs[h].at[sl], act.at[h, sl], sems.at[2 + 2 * n]),
        )

    ready_cot = load(cot_ref, cot, sems.at[0])
    ahead = 2
    ready = [fetch(n) for n in range(ahead)]
    ready_cot.wait()
    out = []
    for n, (h, i) in enumerate(steps):
        if i == 0:
            b1, w2 = None, None
        for copy in ready[n]:
            copy.wait()
        if n + ahead < len(steps):
            ready.append(fetch(n + ahead))
        if n == 0:
            ready_lat = load(lat_ref, lat, lat_sem)
        for q in range(i * blocks // parts, (i + 1) * blocks // parts):
            sl = slice(q * block, (q + 1) * block)
            dact = lax.dot_general(
                cot[q], o_refs[h][...], (((0,), (0,)), ((), ())), preferred_element_type=jnp.float32
            )
            dpre = dact * g[h, sl, :].astype(jnp.float32)
            dpre_v[h, sl, :] = dpre.astype(jnp.bfloat16)
            s = jnp.sum(dpre.reshape(-1, 8, half), axis=0)
            b1 = s if b1 is None else b1 + s
            a = jnp.dot(cot[q], act[h, sl, :], preferred_element_type=jnp.float32)
            w2 = a if w2 is None else w2 + a
        sl = slice(i * tile, (i + 1) * tile)
        out.append(load(dpre_v.at[h, sl], dpre_refs[h].at[sl], out_sems.at[n]))
        if i == parts - 1:
            table[h] = jnp.zeros(table.shape[1:], jnp.float32)
            table[h, :rows, :] = w2
            table[h, variables : variables + 1, :] = jnp.sum(b1, axis=0, keepdims=True)
            if h == 0:
                table[h, variables + 1 : variables + 2, : tail.shape[1]] = tail[...]
    lanes = half // 128
    low = core[0] == 0
    used = -(-(variables + 3) // 8) * lanes
    units = pack.shape[0] // 16
    ready_lat.wait()
    cut = lat.shape[1] // parts
    for m in range(parts):
        at = slice(m * cut, (m + 1) * cut)
        give[at, :] = lax.dot_general(
            lat[:, at], dpre_v[1], (((0,), (0,)), ((), ())), preferred_element_type=jnp.float32
        ).astype(jnp.bfloat16)
        for unit in range(m * units // parts, (m + 1) * units // parts):
            where = slice(16 * unit, 16 * unit + 16)
            if unit >= used:
                pack[where, :] = jnp.zeros((16, pack.shape[1]), jnp.bfloat16)
                continue
            r, c = unit // lanes, unit % lanes
            pieces = []
            for h in range(2):
                piece = table[h, 8 * r : 8 * r + 8, 128 * c : 128 * (c + 1)]
                pieces.append(jnp.concatenate([piece[:, :64], piece[:, 64:]], axis=0))
            first = jnp.where(low, pieces[0], pieces[1])
            second = jnp.where(low, pieces[1], pieces[0])
            pack[where, :] = jnp.concatenate([first, second], axis=1).astype(jnp.bfloat16)
        out.append(load(give.at[at], give_ref.at[at], give_sems.at[m]))
    out.append(load(pack, pack_ref, out_sems.at[len(steps)]))
    for copy in out:
        copy.wait()


def cotangents(core, cot, gs, acts, lat, o_halves, tail, variables):
    width = lat.shape[1]
    points, half = gs[0].shape
    parts = 1
    row = shape((points, half), jnp.bfloat16)
    return pl.pallas_call(
        lambda *refs: cotangent_kernel(variables, parts, *refs),
        in_specs=[pl.BlockSpec(memory_space=pltpu.SMEM), ANY] + [HBM] * 5 + [WHOLE] * 3,
        out_specs=[HBM] * 4,
        out_shape=[row, row, shape((width, 128), jnp.bfloat16), shape((width, half), jnp.bfloat16)],
        scratch_shapes=[
            pltpu.VMEM(cot.shape, jnp.bfloat16),
            pltpu.VMEM((2, points, half), jnp.bfloat16),
            pltpu.VMEM((2, points, half), jnp.bfloat16),
            pltpu.VMEM((2, points, half), jnp.bfloat16),
            pltpu.VMEM((width, 128), jnp.bfloat16),
            pltpu.VMEM((2, width // 8, half), jnp.float32),
            pltpu.VMEM(lat.shape, jnp.bfloat16),
            pltpu.VMEM((width, half), jnp.bfloat16),
            pltpu.SemaphoreType.DMA((1 + 4 * parts,)),
            pltpu.SemaphoreType.DMA,
            pltpu.SemaphoreType.DMA((1 + 2 * parts,)),
            pltpu.SemaphoreType.DMA((parts,)),
        ],
        compiler_params=pltpu.CompilerParams(vmem_limit_bytes=VMEM_BYTES),
        cost_estimate=cost(2 * points * half * (4 * cot.shape[1] + width), points * (12 * half + 2 * width)),
        name="cotangents",
    )(core, cot, *gs, *acts, lat, *o_halves, tail)


def weight_kernel(parts, fused, *refs):
    lat_ref, d_ref = refs[:2]
    got_ref = refs[2] if fused else None
    out_ref, lat, d, acc, total, sems, out_sems = refs[2 + fused :][:7]
    width = lat.shape[1]
    points, half = d.shape
    tile = points // parts
    cut = width // parts
    ready = []
    for i in range(parts):
        sl = slice(i * tile, (i + 1) * tile)
        ready.append((load(d_ref.at[sl], d.at[sl], sems.at[2 * i]), load(lat_ref.at[sl], lat.at[sl], sems.at[2 * i + 1])))
    if fused:
        got = refs[-1]
        ready_got = load(got_ref, got, sems.at[2 * parts])
    out = []
    for i in range(parts):
        for copy in ready[i]:
            copy.wait()
        if fused and i == parts - 1:
            ready_got.wait()
        sl = slice(i * tile, (i + 1) * tile)
        for m in range(parts):
            at = slice(m * cut, (m + 1) * cut)
            term = lax.dot_general(
                lat[sl, at], d[sl, :], (((0,), (0,)), ((), ())), preferred_element_type=jnp.float32
            )
            if i > 0:
                term = term + acc[at, :]
            if i < parts - 1:
                acc[at, :] = term
                continue
            if fused:
                term = term + got[at, :].astype(jnp.float32)
            total[at, :] = term.astype(jnp.bfloat16)
            out.append(load(total.at[at], out_ref.at[at], out_sems.at[m]))
    for copy in out:
        copy.wait()


def weight_half(lat, d, *got):
    points, half = d.shape
    width = lat.shape[1]
    parts = 4
    fused = len(got)
    small = pltpu.VMEM((width, half), jnp.bfloat16)
    return pl.pallas_call(
        lambda *refs: weight_kernel(parts, fused, *refs),
        in_specs=[HBM] * 2 + [ANY] * fused,
        out_specs=ANY,
        out_shape=shape((width, half), jnp.bfloat16),
        scratch_shapes=[
            pltpu.VMEM(lat.shape, jnp.bfloat16),
            pltpu.VMEM(d.shape, jnp.bfloat16),
            pltpu.VMEM((width, half), jnp.float32),
            small,
            pltpu.SemaphoreType.DMA((2 * parts + 1,)),
            pltpu.SemaphoreType.DMA((parts,)),
        ]
        + [small] * fused,
        compiler_params=pltpu.CompilerParams(vmem_limit_bytes=VMEM_BYTES),
        cost_estimate=cost(2 * points * half * width, points * 2 * (width + half) + width * half * 4),
        name="weight_half",
    )(lat, d, *got)


def join_kernel(high, flag, table, mine, out_ref):
    rows, half = mine.shape
    acc = table[0:16, :].astype(jnp.float32)
    for u in range(1, rows // 16):
        acc = acc + table[16 * u : 16 * u + 16, :].astype(jnp.float32)
    small = acc[:8] + acc[8:]
    rest = small - small.astype(jnp.bfloat16).astype(jnp.float32)
    line = lax.broadcasted_iota(jnp.int32, small.shape, 0)
    low = jnp.broadcast_to(rest[high : high + 1], small.shape)
    small = jnp.where((line == high + 1) & (flag[0] == 1), low, small)
    both = jnp.concatenate([small, small], axis=0).astype(jnp.bfloat16)
    for u in range(rows // 16):
        sl = slice(16 * u, 16 * u + 16)
        out_ref[sl, :half] = mine[sl, :]
        out_ref[sl, half:] = both


def join(flag, table, mine, high):
    rows, half = mine.shape
    return pl.pallas_call(
        lambda *refs: join_kernel(high, *refs),
        in_specs=[pl.BlockSpec(memory_space=pltpu.SMEM)] + [WHOLE] * 2,
        out_specs=WHOLE,
        out_shape=shape((rows, half + 128), jnp.bfloat16),
        compiler_params=pltpu.CompilerParams(vmem_limit_bytes=VMEM_SMALL),
        name="join",
    )(flag, table, mine)


def finish_kernel(kappa, share, all_ref, own_ref, w2_ref, b1_ref, b2_ref, loss_ref, tail):
    variables, width = w2_ref.shape
    half = width // 2
    lanes = half // 128
    acc = all_ref[0:16, :half].astype(jnp.float32)
    for u in range(1, all_ref.shape[0] // 16):
        acc = acc + all_ref[16 * u : 16 * u + 16, :half].astype(jnp.float32)
    own_ref[:, :half] = acc[:8] * kappa
    own_ref[:, half:] = acc[8:] * kappa
    for r in range(-(-(variables + 3) // 8)):
        for c in range(lanes):
            u = r * lanes + c
            pair_rows = all_ref[16 * u : 16 * u + 16, half:].astype(jnp.float32)
            a, b = pair_rows[:8], pair_rows[8:]
            for h in range(2):
                piece = jnp.concatenate([a[:, 64 * h : 64 * h + 64], b[:, 64 * h : 64 * h + 64]], axis=1)
                cols = slice(h * half + 128 * c, h * half + 128 * (c + 1))
                low = 8 * r
                keep = min(8, variables - low)
                if keep > 0:
                    w2_ref[low : low + keep, cols] = piece[:keep] * kappa
                at = variables - low
                if 0 <= at < 8:
                    b1_ref[:, cols] = piece[at : at + 1] * kappa
                    tail[:, cols] = piece[at + 1 : at + 2] + piece[at + 2 : at + 3]
    both = tail[:, :half] + tail[:, half:]
    b2_ref[...] = both[:, :128] * kappa
    loss_ref[...] = both[:, 128:256] * share


def finish(everyone, rows, variables, width, kappa, share):
    return pl.pallas_call(
        lambda *refs: finish_kernel(kappa, share, *refs),
        in_specs=[WHOLE],
        out_specs=[WHOLE] * 5,
        out_shape=[
            shape((rows, width), jnp.float32),
            shape((variables, width), jnp.float32),
            shape((1, width), jnp.float32),
            shape((1, 128), jnp.float32),
            shape((1, 128), jnp.float32),
        ],
        scratch_shapes=[pltpu.VMEM((1, width), jnp.float32)],
        compiler_params=pltpu.CompilerParams(vmem_limit_bytes=VMEM_SMALL),
        name="finish",
    )(everyone)


def pair_kernel(plan_ref, f_ref, t_ref, s_ref, cot_ref, tail_ref, b2_ref, l_ref):
    n, v, blk = f_ref.shape
    rounds = plan_ref.shape[0]
    vp = cot_ref.shape[1]
    D = DELTA
    b2_ref[...] = jnp.zeros_like(b2_ref); l_ref[...] = jnp.zeros_like(l_ref)
    cot_ref[...] = jnp.zeros_like(cot_ref)
    RB = 16
    def body(m, _):
        for r0 in range(0, v, RB):
            rs = slice(r0, min(r0+RB, v))
            f = f_ref[m, rs, :]
            sc = s_ref[rs, :]
            d = f - t_ref[rs, :]
            q = d*d + D*D
            inv = lax.rsqrt(q)
            slope = d*inv
            spread = q*inv - D
            ps = jnp.zeros_like(f); pr = jnp.zeros_like(f)
            for r in range(rounds):
                x = f - f_ref[plan_ref[r, m], rs, :]
                y = x*x + D*D
                iv = lax.rsqrt(y)
                ps += x*iv
                pr += y*iv - D
            cot = sc*(slope - ps*(1.0/rounds))
            b2_ref[rs, :] += cot
            l_ref[rs, :] += sc*(spread - pr*(0.5/rounds))
            h = min(RB, v-r0)
            cb = cot.astype(jnp.bfloat16)
            if h < RB:
                cb = jnp.concatenate([cb.astype(jnp.float32), jnp.zeros((RB-h, blk), jnp.float32)]).astype(jnp.bfloat16)
            cot_ref[m, r0:r0+RB, :] = cb
        return 0
    lax.fori_loop(0, n, body, 0)
    tail_ref[:, :128] = jnp.sum(b2_ref[...].T, axis=0, keepdims=True)
    tail_ref[:, 128:] = jnp.full((1, 128), jnp.sum(l_ref[...]), jnp.float32)

def pair(plan, f, t, s):
    n, v, blk = f.shape
    vp = -(-v//16)*16
    vm = pl.BlockSpec(memory_space=pltpu.VMEM)
    return pl.pallas_call(pair_kernel, in_specs=[pl.BlockSpec(memory_space=pltpu.SMEM), vm, vm, vm], out_specs=[vm]*2,
        out_shape=[jax.ShapeDtypeStruct((n,vp,blk),jnp.bfloat16), jax.ShapeDtypeStruct((1,256),jnp.float32)],
        scratch_shapes=[pltpu.VMEM((128,blk),jnp.float32), pltpu.VMEM((v,blk),jnp.float32)],
        compiler_params=pltpu.CompilerParams(vmem_limit_bytes=VMEM_SMALL), name="pair_terms")(plan,f,t,s)


def shards(latent, w_in, b_in, w_out, b_out, targets, var_weight, plan):
    hidden_in = latent[0]
    points, width = hidden_in.shape
    half = width // 2
    variables = w_out.shape[0]
    rounds, members = plan.shape
    member = lax.axis_index("member")
    grid_index = lax.axis_index("grid")
    grid_count = lax.axis_size("grid")
    devices = members * grid_count
    rows = w_in.shape[0]
    total = points * grid_count
    block = points // members
    core = lax.rem(grid_index, 2)
    swap = [(i, i ^ 1) for i in range(devices)]

    halves = jnp.stack([w_in[:, :half], w_in[:, half:]])
    send = jnp.broadcast_to(halves[None], (devices // 2, 2, rows, half))
    w_mine = lax.all_to_all(send.reshape(devices * rows, half), BOTH, 0, 0, tiled=True)
    w_other = lax.ppermute(w_mine, BOTH, swap)

    def part(a, which):
        return lax.dynamic_slice_in_dim(a, which * half, half, a.ndim - 1)

    tall = -(-variables // 8) * 8
    taller = -(-variables // 16) * 16
    out_pad = jnp.pad(w_out, ((0, taller - variables), (0, 0)))
    b_row = b_in[None, :]
    w_halves = (w_mine, w_other)
    b_halves = (part(b_row, core), part(b_row, 1 - core))
    o_halves = (part(out_pad, core), part(out_pad, 1 - core))

    bias = jnp.pad(b_out, (0, tall - variables))[:, None]
    partial = forward_half(
        True, hidden_in, w_mine, b_halves[0], o_halves[0], bias, tall, members
    )
    out = forward_half(
        False, hidden_in, w_other, b_halves[1], o_halves[1], partial, tall, members
    )

    fields = lax.all_to_all(out, "member", 0, 0, tiled=True)
    place = grid_index * points + member * block + jnp.arange(block, dtype=jnp.int32)
    area = jnp.cos(1.4 * (place.astype(jnp.float32) + 0.5) / total)
    scale_map = jnp.pad(area[None, :] * var_weight[:, None], ((0, tall - variables), (0, 0)))
    target = lax.dynamic_slice_in_dim(targets, member * block, block, 1)
    target = jnp.pad(target, ((0, tall - variables), (0, 0)))
    act1, g1 = slope_half(hidden_in, w_other, b_halves[1])
    act0, g0 = slope_half(hidden_in, w_mine, b_halves[0])
    fields, act1, g1 = lax.optimization_barrier((fields, act1, g1))
    cot, tail = pair(plan, fields, target, scale_map)
    back = lax.all_to_all(cot, "member", 0, 0, tiled=True)
    back, act0, g0 = lax.optimization_barrier((back, act0, g0))
    place = member * grid_count + grid_index
    tail_row = variables + 1
    flag = (place // 8 == tail_row // 8).astype(jnp.int32)[None]
    d0, d1, pack, give = cotangents(
        core[None], back, (g0, g1), (act0, act1), hidden_in, o_halves, tail, variables
    )
    tables = lax.all_to_all(pack, BOTH, 0, 0, tiled=True)
    got = lax.ppermute(give, BOTH, swap)
    mine = weight_half(hidden_in, d0, got)
    chunks = join(flag, tables, mine, tail_row % 8)
    chunks, d0, d1 = lax.optimization_barrier((chunks, d0, d1))
    parts = lax.all_to_all(chunks, BOTH, 0, 0, tiled=True)
    grad_hidden = sum(
        jnp.dot(d, w.T, preferred_element_type=jnp.float32) for d, w in zip((d0, d1), w_halves)
    ).astype(jnp.bfloat16)
    kappa = 4.0 / math.sqrt(members * total)
    own_rows, grad_out, grad_bias, grad_b_out, loss = finish(
        parts, rows, variables, width, kappa, 1.0 / (members * total * variables)
    )
    return (
        loss[0, 0],
        grad_hidden[None],
        own_rows,
        grad_bias[0],
        grad_out,
        grad_b_out[0, :variables],
    )


def solution(mesh):
    placed = (
        P("member", "grid", None),
        P(BOTH, None),
        P(),
        P(),
        P(),
        P(None, "grid"),
        P(),
        P(),
    )
    return jax.shard_map(
        shards,
        mesh=mesh,
        in_specs=placed,
        out_specs=(P(), P("member", "grid", None), P(BOTH, None), P(), P(), P()),
        check_vma=False,
    )
```

```python
import math

import jax
import jax.numpy as jnp
from jax import lax
from jax.experimental import pallas as pl
from jax.experimental.pallas import tpu as pltpu
from jax.sharding import PartitionSpec as P

DELTA = 0.25
BOTH = ("member", "grid")
VMEM_BYTES = 60 << 20
VMEM_SMALL = 24 << 20


GELU_A = 0.7978845608028654
GELU_B = 0.044715
WHOLE = pl.BlockSpec(memory_space=pltpu.VMEM)
HBM = pl.BlockSpec(memory_space=pltpu.HBM)
ANY = pl.BlockSpec(memory_space=pl.ANY)


def shape(dims, kind):
    return jax.ShapeDtypeStruct(dims, kind)


def cost(flops, moved, special=0):
    return pl.CostEstimate(flops=flops, bytes_accessed=moved, transcendentals=special)


def load(src, dst, sem):
    copy = pltpu.make_async_copy(src, dst, sem)
    copy.start()
    return copy


def forward_kernel(first, parts, lat, w, b, o, extra, f_ref):
    points = lat.shape[0]
    half = w.shape[1]
    tile = points // parts
    rows, block = f_ref.shape[1:]
    for i in range(parts):
        sl = slice(i * tile, (i + 1) * tile)
        f = None
        for n in range(0, half, 256):
            cols = slice(n, n + 256)
            pre = jnp.dot(lat[sl, :], w[:, cols], preferred_element_type=jnp.float32) + b[:, cols]
            t = jnp.tanh(pre * (GELU_A + (GELU_A * GELU_B) * (pre * pre)))
            act = (pre * (0.5 + 0.5 * t)).astype(jnp.bfloat16)
            g = lax.dot_general(
                o[:, cols], act, (((1,), (1,)), ((), ())), preferred_element_type=jnp.float32
            )
            f = g if f is None else f + g
        for q in range(tile // block):
            at = i * (tile // block) + q
            piece = f[:rows, q * block : (q + 1) * block]
            f_ref[at] = piece + (extra[...] if first else extra[at])


def forward_half(first, lat, w, b, o, extra, rows, blocks):
    points, width = lat.shape
    half = w.shape[1]
    return pl.pallas_call(
        lambda *refs: forward_kernel(first, 2, *refs),
        in_specs=[WHOLE] * 5,
        out_specs=WHOLE,
        out_shape=shape((blocks, rows, points // blocks), jnp.float32),
        compiler_params=pltpu.CompilerParams(vmem_limit_bytes=VMEM_SMALL),
        cost_estimate=cost(2 * points * half * (width + rows), points * 2 * width, points * half),
        name="forward_half",
    )(lat, w, b, o, extra)


def slope_kernel(parts, lat_ref, w_ref, b, act_ref, g_ref, act_v, g_v, lat, w, sems, out_sems):
    points = lat.shape[0]
    half = w.shape[1]
    tile = points // parts
    slices = [slice(i * tile, (i + 1) * tile) for i in range(parts)]

    def fetch(i):
        return load(lat_ref.at[slices[i]], lat.at[slices[i]], sems.at[i])

    ready_w = load(w_ref, w, sems.at[parts])
    ready = [fetch(i) for i in range(parts)]
    ready_w.wait()
    out = []
    for i, sl in enumerate(slices):
        ready[i].wait()
        for n in range(0, half, 256):
            cols = slice(n, n + 256)
            pre = jnp.dot(lat[sl, :], w[:, cols], preferred_element_type=jnp.float32) + b[:, cols]
            sq = pre * pre
            t = jnp.tanh(pre * (GELU_A + (GELU_A * GELU_B) * sq))
            gate = 0.5 + 0.5 * t
            act_v[sl, cols] = (pre * gate).astype(jnp.bfloat16)
            inner = (0.5 * pre) * (1.0 - t * t) * (GELU_A + (3.0 * GELU_A * GELU_B) * sq)
            g_v[sl, cols] = (gate + inner).astype(jnp.bfloat16)
        out.append(load(act_v.at[sl], act_ref.at[sl], out_sems.at[2 * i]))
        out.append(load(g_v.at[sl], g_ref.at[sl], out_sems.at[2 * i + 1]))
    for copy in out:
        copy.wait()


def slope_half(lat, w, b):
    points, width = lat.shape
    half = w.shape[1]
    parts = 4
    return pl.pallas_call(
        lambda *refs: slope_kernel(parts, *refs),
        in_specs=[HBM] * 2 + [WHOLE],
        out_specs=[HBM] * 2,
        out_shape=[shape((points, half), jnp.bfloat16)] * 2,
        scratch_shapes=[
            pltpu.VMEM((points, half), jnp.bfloat16),
            pltpu.VMEM((points, half), jnp.bfloat16),
            pltpu.VMEM((points, width), jnp.bfloat16),
            pltpu.VMEM((width, half), jnp.bfloat16),
            pltpu.SemaphoreType.DMA((parts + 1,)),
            pltpu.SemaphoreType.DMA((2 * parts,)),
        ],
        compiler_params=pltpu.CompilerParams(vmem_limit_bytes=VMEM_BYTES),
        cost_estimate=cost(2 * points * half * width, points * (2 * width + 4 * half), points * half),
        name="slope_half",
    )(lat, w, b)


def cotangent_kernel(variables, parts, *refs):
    core, cot_ref = refs[:2]
    g_refs, act_refs, lat_ref = refs[2:4], refs[4:6], refs[6]
    o_refs, tail = refs[7:9], refs[9]
    dpre_refs, pack_ref, give_ref = refs[10:12], refs[12], refs[13]
    cot, g, act, dpre_v, pack, table, lat, give, sems, lat_sem, out_sems, give_sems = refs[14:]
    blocks, rows, block = cot.shape
    points, half = g_refs[0].shape
    tile = points // parts
    steps = [(h, i) for h in range(2) for i in range(parts)]

    def fetch(n):
        h, i = steps[n]
        sl = slice(i * tile, (i + 1) * tile)
        return (
            load(g_refs[h].at[sl], g.at[h, sl], sems.at[1 + 2 * n]),
            load(act_refs[h].at[sl], act.at[h, sl], sems.at[2 + 2 * n]),
        )

    ready_cot = load(cot_ref, cot, sems.at[0])
    ahead = 2
    ready = [fetch(n) for n in range(ahead)]
    ready_cot.wait()
    out = []
    for n, (h, i) in enumerate(steps):
        if i == 0:
            b1, w2 = None, None
        for copy in ready[n]:
            copy.wait()
        if n + ahead < len(steps):
            ready.append(fetch(n + ahead))
        if n == 0:
            ready_lat = load(lat_ref, lat, lat_sem)
        for q in range(i * blocks // parts, (i + 1) * blocks // parts):
            sl = slice(q * block, (q + 1) * block)
            dact = lax.dot_general(
                cot[q], o_refs[h][...], (((0,), (0,)), ((), ())), preferred_element_type=jnp.float32
            )
            dpre = dact * g[h, sl, :].astype(jnp.float32)
            dpre_v[h, sl, :] = dpre.astype(jnp.bfloat16)
            s = jnp.sum(dpre.reshape(-1, 8, half), axis=0)
            b1 = s if b1 is None else b1 + s
            a = jnp.dot(cot[q], act[h, sl, :], preferred_element_type=jnp.float32)
            w2 = a if w2 is None else w2 + a
        sl = slice(i * tile, (i + 1) * tile)
        out.append(load(dpre_v.at[h, sl], dpre_refs[h].at[sl], out_sems.at[n]))
        if i == parts - 1:
            table[h] = jnp.zeros(table.shape[1:], jnp.float32)
            table[h, :rows, :] = w2
            table[h, variables : variables + 1, :] = jnp.sum(b1, axis=0, keepdims=True)
            if h == 0:
                table[h, variables + 1 : variables + 2, : tail.shape[1]] = tail[...]
    lanes = half // 128
    low = core[0] == 0
    used = -(-(variables + 3) // 8) * lanes
    units = pack.shape[0] // 16
    ready_lat.wait()
    cut = lat.shape[1] // parts
    for m in range(parts):
        at = slice(m * cut, (m + 1) * cut)
        give[at, :] = lax.dot_general(
            lat[:, at], dpre_v[1], (((0,), (0,)), ((), ())), preferred_element_type=jnp.float32
        ).astype(jnp.bfloat16)
        for unit in range(m * units // parts, (m + 1) * units // parts):
            where = slice(16 * unit, 16 * unit + 16)
            if unit >= used:
                pack[where, :] = jnp.zeros((16, pack.shape[1]), jnp.bfloat16)
                continue
            r, c = unit // lanes, unit % lanes
            pieces = []
            for h in range(2):
                piece = table[h, 8 * r : 8 * r + 8, 128 * c : 128 * (c + 1)]
                pieces.append(jnp.concatenate([piece[:, :64], piece[:, 64:]], axis=0))
            first = jnp.where(low, pieces[0], pieces[1])
            second = jnp.where(low, pieces[1], pieces[0])
            pack[where, :] = jnp.concatenate([first, second], axis=1).astype(jnp.bfloat16)
        out.append(load(give.at[at], give_ref.at[at], give_sems.at[m]))
    out.append(load(pack, pack_ref, out_sems.at[len(steps)]))
    for copy in out:
        copy.wait()


def cotangents(core, cot, gs, acts, lat, o_halves, tail, variables):
    width = lat.shape[1]
    points, half = gs[0].shape
    parts = 1
    row = shape((points, half), jnp.bfloat16)
    return pl.pallas_call(
        lambda *refs: cotangent_kernel(variables, parts, *refs),
        in_specs=[pl.BlockSpec(memory_space=pltpu.SMEM), ANY] + [HBM] * 5 + [WHOLE] * 3,
        out_specs=[HBM] * 4,
        out_shape=[row, row, shape((width, 128), jnp.bfloat16), shape((width, half), jnp.bfloat16)],
        scratch_shapes=[
            pltpu.VMEM(cot.shape, jnp.bfloat16),
            pltpu.VMEM((2, points, half), jnp.bfloat16),
            pltpu.VMEM((2, points, half), jnp.bfloat16),
            pltpu.VMEM((2, points, half), jnp.bfloat16),
            pltpu.VMEM((width, 128), jnp.bfloat16),
            pltpu.VMEM((2, width // 8, half), jnp.float32),
            pltpu.VMEM(lat.shape, jnp.bfloat16),
            pltpu.VMEM((width, half), jnp.bfloat16),
            pltpu.SemaphoreType.DMA((1 + 4 * parts,)),
            pltpu.SemaphoreType.DMA,
            pltpu.SemaphoreType.DMA((1 + 2 * parts,)),
            pltpu.SemaphoreType.DMA((parts,)),
        ],
        compiler_params=pltpu.CompilerParams(vmem_limit_bytes=VMEM_BYTES),
        cost_estimate=cost(2 * points * half * (4 * cot.shape[1] + width), points * (12 * half + 2 * width)),
        name="cotangents",
    )(core, cot, *gs, *acts, lat, *o_halves, tail)


def weight_kernel(parts, fused, *refs):
    lat_ref, d_ref = refs[:2]
    got_ref = refs[2] if fused else None
    out_ref, lat, d, acc, total, sems, out_sems = refs[2 + fused :][:7]
    width = lat.shape[1]
    points, half = d.shape
    tile = points // parts
    cut = width // parts
    ready = []
    for i in range(parts):
        sl = slice(i * tile, (i + 1) * tile)
        ready.append((load(d_ref.at[sl], d.at[sl], sems.at[2 * i]), load(lat_ref.at[sl], lat.at[sl], sems.at[2 * i + 1])))
    if fused:
        got = refs[-1]
        ready_got = load(got_ref, got, sems.at[2 * parts])
    out = []
    for i in range(parts):
        for copy in ready[i]:
            copy.wait()
        if fused and i == parts - 1:
            ready_got.wait()
        sl = slice(i * tile, (i + 1) * tile)
        for m in range(parts):
            at = slice(m * cut, (m + 1) * cut)
            term = lax.dot_general(
                lat[sl, at], d[sl, :], (((0,), (0,)), ((), ())), preferred_element_type=jnp.float32
            )
            if i > 0:
                term = term + acc[at, :]
            if i < parts - 1:
                acc[at, :] = term
                continue
            if fused:
                term = term + got[at, :].astype(jnp.float32)
            total[at, :] = term.astype(jnp.bfloat16)
            out.append(load(total.at[at], out_ref.at[at], out_sems.at[m]))
    for copy in out:
        copy.wait()


def weight_half(lat, d, *got):
    points, half = d.shape
    width = lat.shape[1]
    parts = 4
    fused = len(got)
    small = pltpu.VMEM((width, half), jnp.bfloat16)
    return pl.pallas_call(
        lambda *refs: weight_kernel(parts, fused, *refs),
        in_specs=[HBM] * 2 + [ANY] * fused,
        out_specs=ANY,
        out_shape=shape((width, half), jnp.bfloat16),
        scratch_shapes=[
            pltpu.VMEM(lat.shape, jnp.bfloat16),
            pltpu.VMEM(d.shape, jnp.bfloat16),
            pltpu.VMEM((width, half), jnp.float32),
            small,
            pltpu.SemaphoreType.DMA((2 * parts + 1,)),
            pltpu.SemaphoreType.DMA((parts,)),
        ]
        + [small] * fused,
        compiler_params=pltpu.CompilerParams(vmem_limit_bytes=VMEM_BYTES),
        cost_estimate=cost(2 * points * half * width, points * 2 * (width + half) + width * half * 4),
        name="weight_half",
    )(lat, d, *got)


def join_kernel(high, flag, table, mine, out_ref):
    rows, half = mine.shape
    acc = table[0:16, :].astype(jnp.float32)
    for u in range(1, rows // 16):
        acc = acc + table[16 * u : 16 * u + 16, :].astype(jnp.float32)
    small = acc[:8] + acc[8:]
    rest = small - small.astype(jnp.bfloat16).astype(jnp.float32)
    line = lax.broadcasted_iota(jnp.int32, small.shape, 0)
    low = jnp.broadcast_to(rest[high : high + 1], small.shape)
    small = jnp.where((line == high + 1) & (flag[0] == 1), low, small)
    both = jnp.concatenate([small, small], axis=0).astype(jnp.bfloat16)
    for u in range(rows // 16):
        sl = slice(16 * u, 16 * u + 16)
        out_ref[sl, :half] = mine[sl, :]
        out_ref[sl, half:] = both


def join(flag, table, mine, high):
    rows, half = mine.shape
    return pl.pallas_call(
        lambda *refs: join_kernel(high, *refs),
        in_specs=[pl.BlockSpec(memory_space=pltpu.SMEM)] + [WHOLE] * 2,
        out_specs=WHOLE,
        out_shape=shape((rows, half + 128), jnp.bfloat16),
        compiler_params=pltpu.CompilerParams(vmem_limit_bytes=VMEM_SMALL),
        name="join",
    )(flag, table, mine)


def finish_kernel(kappa, share, all_ref, own_ref, w2_ref, b1_ref, b2_ref, loss_ref, tail):
    variables, width = w2_ref.shape
    half = width // 2
    lanes = half // 128
    acc = all_ref[0:16, :half].astype(jnp.float32)
    for u in range(1, all_ref.shape[0] // 16):
        acc = acc + all_ref[16 * u : 16 * u + 16, :half].astype(jnp.float32)
    own_ref[:, :half] = acc[:8] * kappa
    own_ref[:, half:] = acc[8:] * kappa
    for r in range(-(-(variables + 3) // 8)):
        for c in range(lanes):
            u = r * lanes + c
            pair_rows = all_ref[16 * u : 16 * u + 16, half:].astype(jnp.float32)
            a, b = pair_rows[:8], pair_rows[8:]
            for h in range(2):
                piece = jnp.concatenate([a[:, 64 * h : 64 * h + 64], b[:, 64 * h : 64 * h + 64]], axis=1)
                cols = slice(h * half + 128 * c, h * half + 128 * (c + 1))
                low = 8 * r
                keep = min(8, variables - low)
                if keep > 0:
                    w2_ref[low : low + keep, cols] = piece[:keep] * kappa
                at = variables - low
                if 0 <= at < 8:
                    b1_ref[cols] = piece[at] * kappa
                    tail[:, cols] = piece[at + 1 : at + 2] + piece[at + 2 : at + 3]
    both = tail[:, :half] + tail[:, half:]
    b2_ref[...] = both[0, :128] * kappa
    loss_ref[...] = both[:, 128:256] * share


def finish(everyone, rows, variables, width, kappa, share):
    return pl.pallas_call(
        lambda *refs: finish_kernel(kappa, share, *refs),
        in_specs=[WHOLE],
        out_specs=[WHOLE] * 5,
        out_shape=[
            shape((rows, width), jnp.float32),
            shape((variables, width), jnp.float32),
            shape((width,), jnp.float32),
            shape((128,), jnp.float32),
            shape((1, 128), jnp.float32),
        ],
        scratch_shapes=[pltpu.VMEM((1, width), jnp.float32)],
        compiler_params=pltpu.CompilerParams(vmem_limit_bytes=VMEM_SMALL),
        name="finish",
    )(everyone)


def pair_kernel(plan_ref, f_ref, t_ref, s_ref, cot_ref, tail_ref, b2_ref, l_ref):
    n, v, blk = f_ref.shape
    rounds = plan_ref.shape[0]
    vp = cot_ref.shape[1]
    D = DELTA
    b2_ref[...] = jnp.zeros_like(b2_ref); l_ref[...] = jnp.zeros_like(l_ref)
    cot_ref[...] = jnp.zeros_like(cot_ref)
    RB = 16
    def body(m, _):
        for r0 in range(0, v, RB):
            rs = slice(r0, min(r0+RB, v))
            f = f_ref[m, rs, :]
            sc = s_ref[rs, :]
            d = f - t_ref[rs, :]
            q = d*d + D*D
            inv = lax.rsqrt(q)
            slope = d*inv
            spread = q*inv - D
            ps = jnp.zeros_like(f); pr = jnp.zeros_like(f)
            for r in range(rounds):
                x = f - f_ref[plan_ref[r, m], rs, :]
                y = x*x + D*D
                iv = lax.rsqrt(y)
                ps += x*iv
                pr += y*iv - D
            cot = sc*(slope - ps*(1.0/rounds))
            b2_ref[rs, :] += cot
            l_ref[rs, :] += sc*(spread - pr*(0.5/rounds))
            h = min(RB, v-r0)
            cb = cot.astype(jnp.bfloat16)
            if h < RB:
                cb = jnp.concatenate([cb.astype(jnp.float32), jnp.zeros((RB-h, blk), jnp.float32)]).astype(jnp.bfloat16)
            cot_ref[m, r0:r0+RB, :] = cb
        return 0
    lax.fori_loop(0, n, body, 0)
    tail_ref[:, :128] = jnp.sum(b2_ref[...].T, axis=0, keepdims=True)
    tail_ref[:, 128:] = jnp.full((1, 128), jnp.sum(l_ref[...]), jnp.float32)

def pair(plan, f, t, s):
    n, v, blk = f.shape
    vp = -(-v//16)*16
    vm = pl.BlockSpec(memory_space=pltpu.VMEM)
    return pl.pallas_call(pair_kernel, in_specs=[pl.BlockSpec(memory_space=pltpu.SMEM), vm, vm, vm], out_specs=[vm]*2,
        out_shape=[jax.ShapeDtypeStruct((n,vp,blk),jnp.bfloat16), jax.ShapeDtypeStruct((1,256),jnp.float32)],
        scratch_shapes=[pltpu.VMEM((128,blk),jnp.float32), pltpu.VMEM((v,blk),jnp.float32)],
        compiler_params=pltpu.CompilerParams(vmem_limit_bytes=VMEM_SMALL), name="pair_terms")(plan,f,t,s)


def shards(latent, w_in, b_in, w_out, b_out, targets, var_weight, plan):
    hidden_in = latent[0]
    points, width = hidden_in.shape
    half = width // 2
    variables = w_out.shape[0]
    rounds, members = plan.shape
    member = lax.axis_index("member")
    grid_index = lax.axis_index("grid")
    grid_count = lax.axis_size("grid")
    devices = members * grid_count
    rows = w_in.shape[0]
    total = points * grid_count
    block = points // members
    core = lax.rem(grid_index, 2)
    swap = [(i, i ^ 1) for i in range(devices)]

    halves = jnp.stack([w_in[:, :half], w_in[:, half:]])
    send = jnp.broadcast_to(halves[None], (devices // 2, 2, rows, half))
    w_mine = lax.all_to_all(send.reshape(devices * rows, half), BOTH, 0, 0, tiled=True)
    w_other = lax.ppermute(w_mine, BOTH, swap)

    def part(a, which):
        return lax.dynamic_slice_in_dim(a, which * half, half, a.ndim - 1)

    tall = -(-variables // 8) * 8
    taller = -(-variables // 16) * 16
    out_pad = jnp.pad(w_out, ((0, taller - variables), (0, 0)))
    b_row = b_in[None, :]
    w_halves = (w_mine, w_other)
    b_halves = (part(b_row, core), part(b_row, 1 - core))
    o_halves = (part(out_pad, core), part(out_pad, 1 - core))

    bias = jnp.pad(b_out, (0, tall - variables))[:, None]
    partial = forward_half(
        True, hidden_in, w_mine, b_halves[0], o_halves[0], bias, tall, members
    )
    out = forward_half(
        False, hidden_in, w_other, b_halves[1], o_halves[1], partial, tall, members
    )

    fields = lax.all_to_all(out, "member", 0, 0, tiled=True)
    place = grid_index * points + member * block + jnp.arange(block, dtype=jnp.int32)
    area = jnp.cos(1.4 * (place.astype(jnp.float32) + 0.5) / total)
    scale_map = jnp.pad(area[None, :] * var_weight[:, None], ((0, tall - variables), (0, 0)))
    target = lax.dynamic_slice_in_dim(targets, member * block, block, 1)
    target = jnp.pad(target, ((0, tall - variables), (0, 0)))
    act1, g1 = slope_half(hidden_in, w_other, b_halves[1])
    act0, g0 = slope_half(hidden_in, w_mine, b_halves[0])
    fields, act1, g1 = lax.optimization_barrier((fields, act1, g1))
    cot, tail = pair(plan, fields, target, scale_map)
    back = lax.all_to_all(cot, "member", 0, 0, tiled=True)
    back, act0, g0 = lax.optimization_barrier((back, act0, g0))
    place = member * grid_count + grid_index
    tail_row = variables + 1
    flag = (place // 8 == tail_row // 8).astype(jnp.int32)[None]
    d0, d1, pack, give = cotangents(
        core[None], back, (g0, g1), (act0, act1), hidden_in, o_halves, tail, variables
    )
    tables = lax.all_to_all(pack, BOTH, 0, 0, tiled=True)
    got = lax.ppermute(give, BOTH, swap)
    mine = weight_half(hidden_in, d0, got)
    chunks = join(flag, tables, mine, tail_row % 8)
    chunks, d0, d1 = lax.optimization_barrier((chunks, d0, d1))
    parts = lax.all_to_all(chunks, BOTH, 0, 0, tiled=True)
    grad_hidden = sum(
        jnp.dot(d, w.T, preferred_element_type=jnp.float32) for d, w in zip((d0, d1), w_halves)
    ).astype(jnp.bfloat16)
    kappa = 4.0 / math.sqrt(members * total)
    own_rows, grad_out, grad_bias, grad_b_out, loss = finish(
        parts, rows, variables, width, kappa, 1.0 / (members * total * variables)
    )
    return (
        loss[0, 0],
        grad_hidden[None],
        own_rows,
        grad_bias,
        grad_out,
        grad_b_out[:variables],
    )


def solution(mesh):
    placed = (
        P("member", "grid", None),
        P(BOTH, None),
        P(),
        P(),
        P(),
        P(None, "grid"),
        P(),
        P(),
    )
    return jax.shard_map(
        shards,
        mesh=mesh,
        in_specs=placed,
        out_specs=(P(), P("member", "grid", None), P(BOTH, None), P(), P(), P()),
        check_vma=False,
    )
```
